128 devices in a mesh: src: 16 (over z_hi, y, core), rcv: 8 (over z_lo, x).
Axes of the slice: x: 4, y: 4, z: 4 (z_hi: 2, z_lo: 2; z = z_hi * 2 + z_lo), core: 2. Of those that a mesh axis runs over, the one named last changes fastest.
Arguments:
- spectra: bfloat16 [2048, 2, 10, 400], P(('src', 'rcv')), may hold values from -6 to 6
- offsets: int32 [2048, 10], P(('src', 'rcv')), may hold values from 0 to 399
- channel_mask: int32 [2048], P(('src', 'rcv')), may hold values 0 or 1
Outputs:
- correlations: bfloat16 [101, 2048, 2048], P(None, 'src', 'rcv')
The draws below stay inside these ranges and needn't reach their ends.
All inputs are finite; a program needn't handle non-finite values. No bound on the sum of `channel_mask` on one device may be relied on, other than what follows from the above.
Results may differ from the reference program's by a relative error of at most 0.0058.
Values may be sent and summed in bfloat16 or wider, within the bound.
No kernel may reach another device: no remote copies, remote signals or barrier semaphores. Data moves between devices by JAX's collectives and lax.ppermute only.
A program may use at most 128 MiB of HBM per device.

```python
import math
import jax
import jax.numpy as jnp
from jax import lax

W = 10
F = 400
KLO = 6
NT = 12000
HALF = 50
LAGS = 101
C = 2048
N_SRC = 16


def plant(drawn, stream_key, smallest, high):
    shape = drawn.shape
    place = [jax.random.randint(jax.random.fold_in(stream_key, axis), (), 0, shape[axis]) for axis in range(len(shape))]
    drawn = drawn.at[tuple(place)].set(smallest)
    longest = shape.index(max(shape))
    place[longest] = (place[longest] + 1) % shape[longest]
    return drawn.at[tuple(place)].set(high)


def level_of(stream_key, dims, split, low, largest):
    def one(dim, blocks):
        heights = jax.random.uniform(jax.random.fold_in(jax.random.fold_in(stream_key, 6), dim), (blocks,), jnp.float32, low / len(split), largest / len(split))
        return jnp.repeat(jnp.exp(heights), dims[dim] // blocks).reshape((-1,) + (1,) * (len(dims) - dim - 1))

    level = one(*split[0])
    for cut in split[1:]:
        level = level * one(*cut)
    return level


def noise(stream_key, dims, scale, reach, pieces=(), kind=jnp.bfloat16):
    level = level_of(stream_key, dims, pieces, -0.22, 0.18) if pieces else 1.0
    entries = jax.random.normal(stream_key, dims, jnp.float32) * scale * level
    return jnp.minimum(jnp.maximum(entries, -reach), reach).astype(kind)


def setup_inputs(seed: int = 0) -> dict:
    key_of = jax.random.split(jax.random.key(seed), 4)
    spectra = noise(key_of[0], (C, 2, W, F), 1.0, 6.0, ((0, 128),))
    offsets = plant(jax.random.randint(key_of[1], (C, W), 0, 400), jax.random.fold_in(key_of[1], 1), 0, 399).astype(jnp.int32)
    channel_mask = plant((jax.random.randint(key_of[2], (C,), 0, 8) < 7).astype(jnp.int32), jax.random.fold_in(key_of[2], 1), 0, 1)
    return {"spectra": spectra, "offsets": offsets, "channel_mask": channel_mask}


def block_width(total):
    width = 1
    for trial in range(1, 41):
        if total % trial == 0:
            width = trial
    return width

def prepare(spectra, offsets, channel_mask):
    values = spectra.astype(jnp.float32)
    real_part = values[:, 0]
    imag_part = values[:, 1]
    power = lax.optimization_barrier(jnp.mean(real_part * real_part + imag_part * imag_part, axis=-1, keepdims=True))
    scale = lax.rsqrt(power + 1e-06) * channel_mask.astype(jnp.float32)[:, None, None]
    freq = KLO + jnp.arange(F, dtype=jnp.int32)
    turns = offsets[:, :, None] * freq[None, None, :] % NT
    angle = 2.0 * math.pi / NT * turns.astype(jnp.float32)
    cosine = jnp.cos(angle)
    sine = jnp.sin(angle)
    rot_real = (real_part * cosine + imag_part * sine) * scale
    rot_imag = (imag_part * cosine - real_part * sine) * scale
    return jnp.stack([rot_real, rot_imag], 1).astype(jnp.bfloat16)

def lag_table():
    freq = KLO + jnp.arange(F, dtype=jnp.int32)
    shifts = jnp.arange(LAGS, dtype=jnp.int32) - HALF
    turns = shifts[:, None] * freq[None, :] % NT
    angle = 2.0 * math.pi / NT * turns.astype(jnp.float32)
    return jnp.stack([jnp.cos(angle), -jnp.sin(angle)], -1).astype(jnp.bfloat16)

def correlate(rows, cols):
    row_count = rows.shape[0]
    col_count = cols.shape[0]
    width = block_width(F)
    table = lag_table()
    flipped = jnp.stack([cols, jnp.stack([-cols[:, 1], cols[:, 0]], 1)], 1)

    def advance(total, block_index):
        start = block_index * width
        left = lax.dynamic_slice_in_dim(rows, start, width, 3).astype(jnp.float32)
        right = lax.dynamic_slice_in_dim(flipped, start, width, 4).astype(jnp.float32)
        weights = lax.dynamic_slice_in_dim(table, start, width, 1)
        cross = jnp.einsum('icwf,jkcwf->fkij', left, right).astype(jnp.bfloat16)
        total = total + jnp.dot(weights.reshape(LAGS, width * 2), cross.reshape(width * 2, row_count * col_count), preferred_element_type=jnp.float32)
        return (total, None)
    start_total = jnp.zeros((LAGS, row_count * col_count), jnp.float32)
    total = lax.scan(advance, start_total, jnp.arange(F // width, dtype=jnp.int32))[0]
    total = total * (1.0 / math.sqrt(W * F))
    return total.reshape(LAGS, row_count, col_count).astype(jnp.bfloat16)

def reference(spectra, offsets, channel_mask):
    white = prepare(spectra, offsets, channel_mask)
    row_blocks = white.reshape(N_SRC, C // N_SRC, 2, W, F)
    stacked = lax.map(lambda rows: correlate(rows, white), row_blocks)
    return jnp.transpose(stacked, (1, 0, 2, 3)).reshape(LAGS, C, C)
```

```python
import functools
import math

import jax
import jax.numpy as jnp
import numpy as np
from jax import lax
from jax.experimental import pallas as pl
from jax.experimental.pallas import tpu as pltpu
from jax.sharding import PartitionSpec as P

W = 10
F = 400
KLO = 6
NT = 12000
HALF = 50
LAGS = 2 * HALF + 1
LAG_ROWS = 104
FB = 8
NB = F // FB
OWN = 16
MAIN = 16
TILES = NB + -(-NB // 4)
LANES = TILES * 128
GROUP = 32


def unit_circle(turns):
    turns = turns - NT * jnp.floor(turns * (1.0 / NT))
    quarter = jnp.floor(turns * (4.0 / NT) + 0.5)
    a = (turns - (NT // 4) * quarter) * (2.0 * math.pi / NT)
    s = a * a
    sin = a + a * s * (-1 / 6 + s * (1 / 120 + s * (-1 / 5040 + s * (1 / 362880))))
    cos = 1.0 + s * (-0.5 + s * (1 / 24 + s * (-1 / 720 + s * (1 / 40320 + s * (-1 / 3628800)))))
    swap = (quarter == 1.0) | (quarter == 3.0)
    c = jnp.where(swap, sin, cos)
    s = jnp.where(swap, cos, sin)
    c = jnp.where((quarter == 1.0) | (quarter == 2.0), -c, c)
    s = jnp.where((quarter == 2.0) | (quarter == 3.0), -s, s)
    return c, s


def whiten_kernel(mask_ref, spectra_ref, offsets_ref, white_ref, parts):
    freq = (KLO + lax.broadcasted_iota(jnp.int32, (W, F), 1)).astype(jnp.float32)
    eye = lax.broadcasted_iota(jnp.int32, (W, W), 0) == lax.broadcasted_iota(jnp.int32, (W, W), 1)
    parts[3] = jnp.zeros((OWN * 32, 128), jnp.float32)
    for ch in range(OWN):
        re = spectra_ref[ch, 0].astype(jnp.float32)
        im = spectra_ref[ch, 1].astype(jnp.float32)
        power = jnp.sum(re * re + im * im, axis=1, keepdims=True) * (1.0 / F)
        scale = lax.rsqrt(power + 1e-06) * mask_ref[ch].astype(jnp.float32)
        row = jnp.broadcast_to(offsets_ref[ch : ch + 1].astype(jnp.float32), (W, W))
        offset = jnp.sum(jnp.where(eye, row, 0.0), axis=1, keepdims=True)
        c, s = unit_circle(offset * freq)
        out = ((re * c + im * s) * scale, (im * c - re * s) * scale)
        for part in range(2):
            for t in range(4):
                n = min(128, F - 128 * t)
                parts[t, ch * 32 + part * 16 : ch * 32 + part * 16 + W, :n] = out[part][:, 128 * t : 128 * t + n]

    chunk = lax.broadcasted_iota(jnp.int32, (OWN, 128), 1) // 8
    for t in range(4):
        pairs = [parts[t, pl.ds(16 * (m % 2) + m // 2, OWN, stride=32), :] for m in range(2 * W)]
        main, rest = pairs[:MAIN], pairs[MAIN:]
        for values, low, bits in ((main, 0, 4), (rest, 2, 2)):
            for bit in range(bits):
                shift = 8 << (low + bit)
                upper = (chunk >> (low + bit)) % 2 == 1
                for m in range(len(values)):
                    if not m >> bit & 1:
                        a, b = values[m], values[m | 1 << bit]
                        values[m] = jnp.where(upper, pltpu.roll(b, shift, 1), a)
                        values[m | 1 << bit] = jnp.where(upper, b, pltpu.roll(a, 128 - shift, 1))
        for k in range(16):
            if 16 * t + k < NB:
                white_ref[:, (16 * t + k) * 128 : (16 * t + k + 1) * 128] = main[k].astype(jnp.bfloat16)
        for k in range(4):
            tile = NB + 4 * t + k
            if tile < TILES:
                white_ref[:, tile * 128 : (tile + 1) * 128] = rest[k].astype(jnp.bfloat16)


def whiten(spectra, offsets, channel_mask):
    return pl.pallas_call(
        whiten_kernel,
        in_specs=[
            pl.BlockSpec(memory_space=pltpu.SMEM),
            pl.BlockSpec(memory_space=pltpu.VMEM),
            pl.BlockSpec(memory_space=pltpu.VMEM),
        ],
        out_specs=pl.BlockSpec(memory_space=pltpu.VMEM),
        out_shape=jax.ShapeDtypeStruct((OWN, LANES), jnp.bfloat16),
        scratch_shapes=[pltpu.VMEM((4, OWN * 32, 128), jnp.float32)],
    )(channel_mask, spectra, offsets)


def lag_table():
    freq = KLO + np.arange(F)
    shifts = np.arange(LAGS) - HALF
    angle = 2.0 * math.pi / NT * ((shifts[:, None] * freq[None, :]) % NT)
    table = np.stack([np.cos(angle), -np.sin(angle)], 1).reshape(LAGS, 2, NB, FB)
    table = table.transpose(0, 2, 1, 3).reshape(LAGS, 2 * F)
    return np.pad(table, ((0, LAG_ROWS - LAGS), (0, 0)))


def correlate_kernel(n_rows, n_cols, place_ref, *refs):
    row_refs, refs = refs[:n_rows], refs[n_rows:]
    col_refs, refs = refs[:n_cols], refs[n_cols:]
    table_ref, out_ref, cols, cols_t, rows, turned, cross, lagged = refs
    step = pl.program_id(0)
    lane = lax.broadcasted_iota(jnp.int32, (8, 128), 1)
    same_bin = (lane % 8) == lax.broadcasted_iota(jnp.int32, (8, 128), 0)

    @pl.when(step == 0)
    def _():
        for k, ref in enumerate(col_refs):
            cols[pl.ds(pl.multiple_of(place_ref[n_rows + k] * OWN, OWN), OWN), :] = ref[...]

        def turn(values, shift):
            odd = (lax.broadcasted_iota(jnp.int32, values.shape, 1) // shift) % 2 == 1
            return jnp.where(odd, -pltpu.roll(values, shift, 1), pltpu.roll(values, 128 - shift, 1))

        for k, ref in enumerate(row_refs):
            at = pl.ds(pl.multiple_of(place_ref[k] * OWN, OWN), OWN)

            @pl.loop(0, NB)
            def _(t):
                o = pl.ds(pl.multiple_of(t * 128, 128), 128)
                r = ref[:, o].astype(jnp.float32)
                rows[at, o] = r
                turned[at, o] = turn(r, 8)

            @pl.loop(NB, TILES)
            def _(t):
                o = pl.ds(pl.multiple_of(t * 128, 128), 128)
                r = ref[:, o].astype(jnp.float32)
                rows[at, o] = r
                turned[at, o] = turn(r, 32)

        @pl.loop(0, TILES)
        def _(t):
            o = pl.ds(pl.multiple_of(t * 128, 128), 128)
            cols_t[o, :] = cols[:, o].T

    base = pl.multiple_of(step * GROUP, GROUP)

    @pl.loop(0, NB)
    def _(b):
        mo = pl.ds(pl.multiple_of(b * 128, 128), 128)
        ro = pl.ds(pl.multiple_of((NB + b // 4) * 128, 128), 128)
        right = jnp.concatenate([cols_t[mo, :], cols_t[ro, :]], 0)
        same_rest = same_bin & ((lane // 8) % 4 == b % 4)
        for g in range(GROUP // 8):
            at = pl.ds(pl.multiple_of(base + g * 8, 8), 8)
            loaded = [rows[at, mo], turned[at, mo], rows[at, ro], turned[at, ro]]
            left = []
            for u in range(8):
                v = [jnp.broadcast_to(x[u : u + 1], (8, 128)) for x in loaded]
                m = jnp.concatenate([jnp.where(same_bin, v[0], 0.0), jnp.where(same_bin, v[1], 0.0)], 0)
                r = jnp.concatenate([jnp.where(same_rest, v[2], 0.0), jnp.where(same_rest, v[3], 0.0)], 0)
                left.append(jnp.concatenate([m.astype(jnp.bfloat16), r.astype(jnp.bfloat16)], 1))
            product = jnp.dot(jnp.concatenate(left, 0), right, preferred_element_type=jnp.float32)
            product = product.astype(jnp.bfloat16)
            for u in range(8):
                cross[g * 8 + u, pl.ds(pl.multiple_of(b * 16, 16), 16), :] = product[u * 16 : u * 16 + 16]

    @pl.loop(0, GROUP // 16)
    def _(g):
        for u in range(16):
            z = jnp.dot(table_ref[...], cross[g * 16 + u], preferred_element_type=jnp.float32)
            for h in range(2):
                lagged[h, u * LAG_ROWS : (u + 1) * LAG_ROWS, :] = z[:, h * 128 : (h + 1) * 128]
        at = pl.ds(pl.multiple_of(g * 16, 16), 16)
        for lag in range(LAGS):
            for h in range(2):
                v = lagged[h, pl.ds(lag, 16, stride=LAG_ROWS), :] * (1.0 / math.sqrt(W * F))
                out_ref[lag, at, h * 128 : (h + 1) * 128] = v.astype(jnp.bfloat16)


def correlate(places, row_blocks, col_blocks):
    n, m = OWN * len(row_blocks), OWN * len(col_blocks)
    whole = pl.BlockSpec((OWN, LANES), lambda s: (0, 0))
    return pl.pallas_call(
        functools.partial(correlate_kernel, len(row_blocks), len(col_blocks)),
        grid=(n // GROUP,),
        in_specs=[pl.BlockSpec(memory_space=pltpu.SMEM)]
        + [whole] * (len(row_blocks) + len(col_blocks))
        + [pl.BlockSpec((LAG_ROWS, 2 * F), lambda s: (0, 0))],
        out_specs=pl.BlockSpec((LAGS, GROUP, m), lambda s: (0, s, 0)),
        out_shape=jax.ShapeDtypeStruct((LAGS, n, m), jnp.bfloat16),
        scratch_shapes=[
            pltpu.VMEM((m, LANES), jnp.bfloat16),
            pltpu.VMEM((LANES, m), jnp.bfloat16),
            pltpu.VMEM((n, LANES), jnp.float32),
            pltpu.VMEM((n, LANES), jnp.float32),
            pltpu.VMEM((GROUP, 2 * F, m), jnp.bfloat16),
            pltpu.VMEM((2, 16 * LAG_ROWS, 128), jnp.float32),
        ],
        compiler_params=pltpu.CompilerParams(vmem_limit_bytes=60 * 1024 * 1024),
    )(places, *row_blocks, *col_blocks, jnp.asarray(lag_table(), jnp.bfloat16))


def gather8(block, move):
    side = move(block, 0, 1)
    found = {(0, 0): block, (0, 1): side}
    found[-1, 0] = move(block, 1, 0)
    found[1, 0] = move(block, -1, 0)
    found[2, 0] = move(found[-1, 0], 1, 0)
    found[-1, 1] = move(side, 1, 0)
    found[1, 1] = move(side, -1, 0)
    found[2, 1] = move(found[2, 0], 0, 1)
    return found


def body(spectra, offsets, channel_mask):
    white = whiten(spectra, offsets, channel_mask)
    p, src = lax.axis_index("rcv"), lax.axis_index("src")
    q, core = src // 2, src % 2

    def step(index, ring, side):
        return (index ^ (4 * side)) & 4 | (index + ring) & 3

    def over_rcv(value, ring, side):
        return lax.ppermute(value, "rcv", [(i, step(i, ring, side)) for i in range(8)])

    def over_src(value, ring, side):
        return lax.ppermute(value, "src", [(i, 2 * step(i // 2, ring, side) + i % 2) for i in range(16)])

    def other_core(value):
        return lax.ppermute(value, "src", [(i, i ^ 1) for i in range(16)])

    flip = [((i * 2 + k) * 8 + j, (j * 2 + k) * 8 + i) for i in range(8) for k in range(2) for j in range(8)]
    turned = lax.ppermute(white, ("src", "rcv"), flip)
    rows = gather8(white, over_rcv)
    cols = gather8(turned, over_src)
    swapped = {key: other_core(value) for key, value in cols.items()}
    places = [step(p, *key) for key in rows]
    places += [core * 8 + step(q, *key) for key in cols]
    places += [(1 - core) * 8 + step(q, *key) for key in swapped]
    places = jnp.stack(places).astype(jnp.int32)
    return correlate(places, list(rows.values()), list(cols.values()) + list(swapped.values()))


def solution(mesh):
    in_specs = (P(("src", "rcv"), None, None, None), P(("src", "rcv"), None), P(("src", "rcv")))
    out_specs = P(None, "src", "rcv")
    return jax.shard_map(body, mesh=mesh, in_specs=in_specs, out_specs=out_specs, check_vma=False)
```

```python
import functools
import math

import jax
import jax.numpy as jnp
import numpy as np
from jax import lax
from jax.experimental import pallas as pl
from jax.experimental.pallas import tpu as pltpu
from jax.sharding import PartitionSpec as P

W = 10
F = 400
KLO = 6
NT = 12000
HALF = 50
LAGS = 2 * HALF + 1
LAG_ROWS = 104
LAG_TILE = 112
FB = 8
NB = F // FB
OWN = 16
MAIN = 16
TILES = NB + -(-NB // 4)
LANES = TILES * 128
HALF_ROWS = 64
DEPTH = 4
LAG = 6


def unit_circle(turns):
    turns = turns - NT * jnp.floor(turns * (1.0 / NT))
    quarter = jnp.floor(turns * (4.0 / NT) + 0.5)
    a = (turns - (NT // 4) * quarter) * (2.0 * math.pi / NT)
    s = a * a
    sin = a + a * s * (-1 / 6 + s * (1 / 120 + s * (-1 / 5040 + s * (1 / 362880))))
    cos = 1.0 + s * (-0.5 + s * (1 / 24 + s * (-1 / 720 + s * (1 / 40320 + s * (-1 / 3628800)))))
    swap = (quarter == 1.0) | (quarter == 3.0)
    c = jnp.where(swap, sin, cos)
    s = jnp.where(swap, cos, sin)
    c = jnp.where((quarter == 1.0) | (quarter == 2.0), -c, c)
    s = jnp.where((quarter == 2.0) | (quarter == 3.0), -s, s)
    return c, s


def whiten_kernel(mask_ref, spectra_ref, offsets_ref, white_ref, parts):
    freq = (KLO + lax.broadcasted_iota(jnp.int32, (W, F), 1)).astype(jnp.float32)
    eye = lax.broadcasted_iota(jnp.int32, (W, W), 0) == lax.broadcasted_iota(jnp.int32, (W, W), 1)
    parts[3] = jnp.zeros((OWN * 32, 128), jnp.float32)
    for ch in range(OWN):
        re = spectra_ref[ch, 0].astype(jnp.float32)
        im = spectra_ref[ch, 1].astype(jnp.float32)
        power = jnp.sum(re * re + im * im, axis=1, keepdims=True) * (1.0 / F)
        scale = lax.rsqrt(power + 1e-06) * mask_ref[ch].astype(jnp.float32)
        row = jnp.broadcast_to(offsets_ref[ch : ch + 1].astype(jnp.float32), (W, W))
        offset = jnp.sum(jnp.where(eye, row, 0.0), axis=1, keepdims=True)
        c, s = unit_circle(offset * freq)
        out = ((re * c + im * s) * scale, (im * c - re * s) * scale)
        for part in range(2):
            for t in range(4):
                n = min(128, F - 128 * t)
                parts[t, ch * 32 + part * 16 : ch * 32 + part * 16 + W, :n] = out[part][:, 128 * t : 128 * t + n]

    chunk = lax.broadcasted_iota(jnp.int32, (OWN, 128), 1) // 8
    for t in range(4):
        pairs = [parts[t, pl.ds(16 * (m % 2) + m // 2, OWN, stride=32), :] for m in range(2 * W)]
        main, rest = pairs[:MAIN], pairs[MAIN:]
        for values, low, bits in ((main, 0, 4), (rest, 2, 2)):
            for bit in range(bits):
                shift = 8 << (low + bit)
                upper = (chunk >> (low + bit)) % 2 == 1
                for m in range(len(values)):
                    if not m >> bit & 1:
                        a, b = values[m], values[m | 1 << bit]
                        values[m] = jnp.where(upper, pltpu.roll(b, shift, 1), a)
                        values[m | 1 << bit] = jnp.where(upper, b, pltpu.roll(a, 128 - shift, 1))
        for k in range(16):
            if 16 * t + k < NB:
                white_ref[:, (16 * t + k) * 128 : (16 * t + k + 1) * 128] = main[k].astype(jnp.bfloat16)
        for k in range(4):
            tile = NB + 4 * t + k
            if tile < TILES:
                white_ref[:, tile * 128 : (tile + 1) * 128] = rest[k].astype(jnp.bfloat16)


def whiten(spectra, offsets, channel_mask):
    return pl.pallas_call(
        whiten_kernel,
        in_specs=[
            pl.BlockSpec(memory_space=pltpu.SMEM),
            pl.BlockSpec(memory_space=pltpu.VMEM),
            pl.BlockSpec(memory_space=pltpu.VMEM),
        ],
        out_specs=pl.BlockSpec(memory_space=pltpu.VMEM),
        out_shape=jax.ShapeDtypeStruct((OWN, LANES), jnp.bfloat16),
        scratch_shapes=[pltpu.VMEM((4, OWN * 32, 128), jnp.float32)],
    )(channel_mask, spectra, offsets)


def lag_tables(offsets):
    freq = KLO + np.arange(F)
    shifts = np.arange(LAGS) - HALF
    angle = 2.0 * math.pi / NT * ((shifts[:, None] * freq[None, :]) % NT)
    table = np.stack([np.cos(angle), -np.sin(angle)], 1).reshape(LAGS, 2, NB, FB)
    table = table.transpose(0, 2, 1, 3).reshape(LAGS, 2 * F)
    table = np.pad(table, ((0, LAG_TILE - LAGS), (0, 0)))
    tiles, done = [], 0
    for at in offsets:
        tile = table[:, at : at + 256].copy()
        tile[:, : done - at] = 0
        tiles.append(tile)
        done = at + 256
    return np.stack(tiles)


def tile_offsets(rows):
    return [min(at, rows - 256) for at in range(0, rows, 256)]


def correlate_kernel(n_rows, n_cols, place_ref, *refs):
    row_refs, refs = refs[:n_rows], refs[n_rows:]
    col_refs, refs = refs[:n_cols], refs[n_cols:]
    table_ref, out_ref, cols, cross, lagged, staged, sems = refs
    lane = lax.broadcasted_iota(jnp.int32, (16, 128), 1)
    same_bin = (lane % 8) == lax.broadcasted_iota(jnp.int32, (16, 128), 0) % 8
    zero = jnp.zeros((), jnp.bfloat16)
    groups = HALF_ROWS // 8

    for k, ref in enumerate(col_refs):
        cols[pl.ds(pl.multiple_of(place_ref[n_rows + k] * OWN, OWN), OWN), :] = ref[...]

    def turn(values, shift):
        odd = (lax.broadcasted_iota(jnp.int32, values.shape, 1) // shift) % 2 == 1
        return jnp.where(odd, -pltpu.roll(values, shift, 1), pltpu.roll(values, 128 - shift, 1))

    def lanes_of(b):
        return pl.ds(pl.multiple_of(b * 128, 128), 128), pl.ds(pl.multiple_of((NB + b // 4) * 128, 128), 128)

    def cross_of(half, *accs):
        def push(b, mxu):
            mo, ro = lanes_of(b)
            right = jnp.concatenate([cols[:, mo], cols[:, ro]], 1)
            pltpu.matmul_push_rhs(right, 0, mxu, transpose=True)

        def left(b, k, same_rest):
            mo, ro = lanes_of(b)
            ref = row_refs[half * (HALF_ROWS // OWN) + k // 2]
            at = slice(k % 2 * 8, k % 2 * 8 + 8)
            m, r = ref[at, mo].astype(jnp.float32), ref[at, ro].astype(jnp.float32)
            loaded = [m, turn(m, 8), r, turn(r, 32)]
            parts = []
            for u in range(8):
                v = [jnp.broadcast_to(x[u : u + 1], (8, 128)) for x in loaded]
                m = jnp.where(same_bin, jnp.concatenate(v[:2], 0).astype(jnp.bfloat16), zero)
                r = jnp.where(same_rest, jnp.concatenate(v[2:], 0).astype(jnp.bfloat16), zero)
                parts.append(jnp.concatenate([m, r], 1))
            return jnp.concatenate(parts, 0)

        def acc_of(k):
            return accs[DEPTH * (k % 2) + k // 2 % DEPTH]

        def pop(b, k):
            product = pltpu.matmul_pop(acc_of(k)).astype(jnp.bfloat16)
            at = pl.ds(pl.multiple_of(b * 16, 16), 16)
            for u in range(8):
                cross[k * 8 + u, at, :] = product[u * 16 : u * 16 + 16]

        def block(b, first, last):
            same_rest = same_bin & ((lane // 8) % 4 == b % 4)
            for k in range(groups):
                pltpu.matmul_acc_lhs(acc_of(k), left(b, k, same_rest), 0 if k < 2 else None)
                if not last and 2 <= k < 4:
                    push(b + 1, k % 2)
                if k >= LAG:
                    pop(b, k - LAG)
                elif not first:
                    pop(b - 1, k - LAG + groups)

        push(0, 0)
        push(0, 1)
        block(0, True, False)
        pl.loop(1, NB - 1)(lambda b: block(b, False, False))
        block(NB - 1, False, True)
        for k in range(groups - LAG, groups):
            pop(NB - 1, k)

    def out_copy(slot, k):
        at = pl.ds(pl.multiple_of(place_ref[k] * OWN, OWN), OWN)
        return pltpu.make_async_copy(staged.at[slot], out_ref.at[:, at, :], sems.at[slot])

    offsets = tile_offsets(2 * F)

    def lags_of(half, *accs):
        for g in range(HALF_ROWS // OWN):
            k = half * (HALF_ROWS // OWN) + g

            def pop(u):
                z = pltpu.matmul_pop(accs[u % 8])
                for h in range(2):
                    lagged[h, u * LAG_ROWS : (u + 1) * LAG_ROWS, :] = z[:LAG_ROWS, h * 128 : (h + 1) * 128]

            for u in range(0, OWN, 2):
                for t, at in enumerate(offsets):
                    for v in (u, u + 1):
                        pltpu.matmul_push_rhs(cross[g * OWN + v, at : at + 256, :], t % 2, v % 2)
                    for v in (u, u + 1):
                        pltpu.matmul_acc_lhs(accs[v % 8], table_ref[t], t % 2)
                if u >= 4:
                    pop(u - 4)
                    pop(u - 3)
            for u in range(OWN - 4, OWN):
                pop(u)
            slot = k % 2
            if k >= 2:
                out_copy(slot, k - 2).wait()
            for lag in range(LAGS):
                for h in range(2):
                    v = lagged[h, pl.ds(lag, OWN, stride=LAG_ROWS), :] * (1.0 / math.sqrt(W * F))
                    staged[slot, lag, :, h * 128 : (h + 1) * 128] = v.astype(jnp.bfloat16)
            out_copy(slot, k).start()

    for half in range(n_rows * OWN // HALF_ROWS):
        pl.run_scoped(
            functools.partial(cross_of, half),
            *[pltpu.ACC(mxu)((128, 256), jnp.float32) for mxu in [0] * DEPTH + [1] * DEPTH],
        )
        pl.run_scoped(
            functools.partial(lags_of, half),
            *[pltpu.ACC(mxu)((LAG_TILE, 256), jnp.float32) for mxu in (0, 1) * 4],
        )
    for k in range(n_rows - 2, n_rows):
        out_copy(k % 2, k).wait()


def correlate(places, row_blocks, col_blocks):
    n, m = OWN * len(row_blocks), OWN * len(col_blocks)
    vmem = pl.BlockSpec(memory_space=pltpu.VMEM)
    tables = jnp.asarray(lag_tables(tile_offsets(2 * F)), jnp.bfloat16)
    return pl.pallas_call(
        functools.partial(correlate_kernel, len(row_blocks), len(col_blocks)),
        in_specs=[pl.BlockSpec(memory_space=pltpu.SMEM)] + [vmem] * (len(row_blocks) + len(col_blocks) + 1),
        out_specs=pl.BlockSpec(memory_space=pl.ANY),
        out_shape=jax.ShapeDtypeStruct((LAGS, n, m), jnp.bfloat16),
        scratch_shapes=[
            pltpu.VMEM((m, LANES), jnp.bfloat16),
            pltpu.VMEM((HALF_ROWS, 2 * F, m), jnp.bfloat16),
            pltpu.VMEM((2, OWN * LAG_ROWS, 128), jnp.float32),
            pltpu.VMEM((2, LAGS, OWN, m), jnp.bfloat16),
            pltpu.SemaphoreType.DMA((2,)),
        ],
        compiler_params=pltpu.CompilerParams(vmem_limit_bytes=56 * 1024 * 1024),
    )(places, *row_blocks, *col_blocks, tables)


def gather8(block, move):
    side = move(block, 0, 1)
    found = {(0, 0): block, (0, 1): side}
    found[-1, 0] = move(block, 1, 0)
    found[1, 0] = move(block, -1, 0)
    found[2, 0] = move(found[-1, 0], 1, 0)
    found[-1, 1] = move(side, 1, 0)
    found[1, 1] = move(side, -1, 0)
    found[2, 1] = move(found[2, 0], 0, 1)
    return found


def body(spectra, offsets, channel_mask):
    white = whiten(spectra, offsets, channel_mask)
    p, src = lax.axis_index("rcv"), lax.axis_index("src")
    q, core = src // 2, src % 2

    def step(index, ring, side):
        return (index ^ (4 * side)) & 4 | (index + ring) & 3

    def over_rcv(value, ring, side):
        return lax.ppermute(value, "rcv", [(i, step(i, ring, side)) for i in range(8)])

    def over_src(value, ring, side):
        return lax.ppermute(value, "src", [(i, 2 * step(i // 2, ring, side) + i % 2) for i in range(16)])

    def other_core(value):
        return lax.ppermute(value, "src", [(i, i ^ 1) for i in range(16)])

    flip = [((i * 2 + k) * 8 + j, (j * 2 + k) * 8 + i) for i in range(8) for k in range(2) for j in range(8)]
    turned = lax.ppermute(white, ("src", "rcv"), flip)
    rows = gather8(white, over_rcv)
    cols = gather8(turned, over_src)
    swapped = {key: other_core(value) for key, value in cols.items()}
    places = [step(p, *key) for key in rows]
    places += [core * 8 + step(q, *key) for key in cols]
    places += [(1 - core) * 8 + step(q, *key) for key in swapped]
    places = jnp.stack(places).astype(jnp.int32)
    return correlate(places, list(rows.values()), list(cols.values()) + list(swapped.values()))


def solution(mesh):
    in_specs = (P(("src", "rcv"), None, None, None), P(("src", "rcv"), None), P(("src", "rcv")))
    out_specs = P(None, "src", "rcv")
    return jax.shard_map(body, mesh=mesh, in_specs=in_specs, out_specs=out_specs, check_vma=False)
```

```python
import functools
import math

import jax
import jax.numpy as jnp
import numpy as np
from jax import lax
from jax.experimental import pallas as pl
from jax.experimental.pallas import tpu as pltpu
from jax.sharding import PartitionSpec as P

W = 10
F = 400
KLO = 6
NT = 12000
HALF = 50
LAGS = 2 * HALF + 1
LAG_ROWS = 104
LAG_TILE = 112
FB = 8
NB = F // FB
OWN = 16
MAIN = 16
TILES = NB + -(-NB // 4)
LANES = TILES * 128
HALF_ROWS = 64
DEPTH = 4
LAG = 6


def unit_circle(turns):
    turns = turns - NT * jnp.floor(turns * (1.0 / NT))
    quarter = jnp.floor(turns * (4.0 / NT) + 0.5)
    a = (turns - (NT // 4) * quarter) * (2.0 * math.pi / NT)
    s = a * a
    sin = a + a * s * (-1 / 6 + s * (1 / 120 + s * (-1 / 5040 + s * (1 / 362880))))
    cos = 1.0 + s * (-0.5 + s * (1 / 24 + s * (-1 / 720 + s * (1 / 40320 + s * (-1 / 3628800)))))
    swap = (quarter == 1.0) | (quarter == 3.0)
    c = jnp.where(swap, sin, cos)
    s = jnp.where(swap, cos, sin)
    c = jnp.where((quarter == 1.0) | (quarter == 2.0), -c, c)
    s = jnp.where((quarter == 2.0) | (quarter == 3.0), -s, s)
    return c, s


def whiten_kernel(mask_ref, spectra_ref, offsets_ref, white_ref, parts):
    freq = (KLO + lax.broadcasted_iota(jnp.int32, (W, F), 1)).astype(jnp.float32)
    eye = lax.broadcasted_iota(jnp.int32, (W, W), 0) == lax.broadcasted_iota(jnp.int32, (W, W), 1)
    parts[3] = jnp.zeros((OWN * 32, 128), jnp.float32)
    for ch in range(OWN):
        re = spectra_ref[ch, 0].astype(jnp.float32)
        im = spectra_ref[ch, 1].astype(jnp.float32)
        power = jnp.sum(re * re + im * im, axis=1, keepdims=True) * (1.0 / F)
        scale = lax.rsqrt(power + 1e-06) * mask_ref[ch].astype(jnp.float32)
        row = jnp.broadcast_to(offsets_ref[ch : ch + 1].astype(jnp.float32), (W, W))
        offset = jnp.sum(jnp.where(eye, row, 0.0), axis=1, keepdims=True)
        c, s = unit_circle(offset * freq)
        out = ((re * c + im * s) * scale, (im * c - re * s) * scale)
        for part in range(2):
            for t in range(4):
                n = min(128, F - 128 * t)
                parts[t, ch * 32 + part * 16 : ch * 32 + part * 16 + W, :n] = out[part][:, 128 * t : 128 * t + n]

    chunk = lax.broadcasted_iota(jnp.int32, (OWN, 128), 1) // 8
    for t in range(4):
        pairs = [parts[t, pl.ds(16 * (m % 2) + m // 2, OWN, stride=32), :] for m in range(2 * W)]
        main, rest = pairs[:MAIN], pairs[MAIN:]
        for values, low, bits in ((main, 0, 4), (rest, 2, 2)):
            for bit in range(bits):
                shift = 8 << (low + bit)
                upper = (chunk >> (low + bit)) % 2 == 1
                for m in range(len(values)):
                    if not m >> bit & 1:
                        a, b = values[m], values[m | 1 << bit]
                        values[m] = jnp.where(upper, pltpu.roll(b, shift, 1), a)
                        values[m | 1 << bit] = jnp.where(upper, b, pltpu.roll(a, 128 - shift, 1))
        for k in range(16):
            if 16 * t + k < NB:
                white_ref[:, (16 * t + k) * 128 : (16 * t + k + 1) * 128] = main[k].astype(jnp.bfloat16)
        for k in range(4):
            tile = NB + 4 * t + k
            if tile < TILES:
                white_ref[:, tile * 128 : (tile + 1) * 128] = rest[k].astype(jnp.bfloat16)


def whiten(spectra, offsets, channel_mask):
    return pl.pallas_call(
        whiten_kernel,
        in_specs=[
            pl.BlockSpec(memory_space=pltpu.SMEM),
            pl.BlockSpec(memory_space=pltpu.VMEM),
            pl.BlockSpec(memory_space=pltpu.VMEM),
        ],
        out_specs=pl.BlockSpec(memory_space=pltpu.VMEM),
        out_shape=jax.ShapeDtypeStruct((OWN, LANES), jnp.bfloat16),
        scratch_shapes=[pltpu.VMEM((4, OWN * 32, 128), jnp.float32)],
    )(channel_mask, spectra, offsets)


def lag_tables(offsets):
    freq = KLO + np.arange(F)
    shifts = np.arange(LAGS) - HALF
    angle = 2.0 * math.pi / NT * ((shifts[:, None] * freq[None, :]) % NT)
    table = np.stack([np.cos(angle), -np.sin(angle)], 1).reshape(LAGS, 2, NB, FB)
    table = table.transpose(0, 2, 1, 3).reshape(LAGS, 2 * F)
    table = np.pad(table, ((0, LAG_TILE - LAGS), (0, 0)))
    tiles, done = [], 0
    for at in offsets:
        tile = table[:, at : at + 256].copy()
        tile[:, : done - at] = 0
        tiles.append(tile)
        done = at + 256
    return np.stack(tiles)


def tile_offsets(rows):
    return [min(at, rows - 256) for at in range(0, rows, 256)]


def correlate_kernel(n_rows, n_cols, place_ref, *refs):
    row_refs, refs = refs[:n_rows], refs[n_rows:]
    col_refs, refs = refs[:n_cols], refs[n_cols:]
    table_ref, out_ref, cols, cross, lagged, staged, sems = refs
    lane = lax.broadcasted_iota(jnp.int32, (16, 128), 1)
    same_bin = (lane % 8) == lax.broadcasted_iota(jnp.int32, (16, 128), 0) % 8
    zero = jnp.zeros((), jnp.bfloat16)
    groups = HALF_ROWS // 8

    for k, ref in enumerate(col_refs):
        cols[pl.ds(pl.multiple_of(place_ref[n_rows + k] * OWN, OWN), OWN), :] = ref[...]

    def turn(values, shift):
        odd = (lax.broadcasted_iota(jnp.int32, values.shape, 1) // shift) % 2 == 1
        return jnp.where(odd, -pltpu.roll(values, shift, 1), pltpu.roll(values, 128 - shift, 1))

    def lanes_of(b):
        return pl.ds(pl.multiple_of(b * 128, 128), 128), pl.ds(pl.multiple_of((NB + b // 4) * 128, 128), 128)

    def cross_of(half, *accs):
        def push(b, mxu):
            mo, ro = lanes_of(b)
            right = jnp.concatenate([cols[:, mo], cols[:, ro]], 1)
            pltpu.matmul_push_rhs(right, 0, mxu, transpose=True)

        def left(b, k, same_rest):
            mo, ro = lanes_of(b)
            ref = row_refs[half * (HALF_ROWS // OWN) + k // 2]
            at = slice(k % 2 * 8, k % 2 * 8 + 8)
            m, r = ref[at, mo].astype(jnp.float32), ref[at, ro].astype(jnp.float32)
            loaded = [m, turn(m, 8), r, turn(r, 32)]
            parts = []
            for u in range(8):
                v = [jnp.broadcast_to(x[u : u + 1], (8, 128)) for x in loaded]
                m = jnp.where(same_bin, jnp.concatenate(v[:2], 0).astype(jnp.bfloat16), zero)
                r = jnp.where(same_rest, jnp.concatenate(v[2:], 0).astype(jnp.bfloat16), zero)
                parts.append(jnp.concatenate([m, r], 1))
            return jnp.concatenate(parts, 0)

        def acc_of(k):
            return accs[DEPTH * (k % 2) + k // 2 % DEPTH]

        def pop(b, k):
            product = pltpu.matmul_pop(acc_of(k)).astype(jnp.bfloat16)
            at = pl.ds(pl.multiple_of(b * 16, 16), 16)
            for u in range(8):
                cross[k * 8 + u, at, :] = product[u * 16 : u * 16 + 16]

        def block(b, first, last):
            same_rest = same_bin & ((lane // 8) % 4 == b % 4)
            for k in range(groups):
                pltpu.matmul_acc_lhs(acc_of(k), left(b, k, same_rest), 0 if k < 2 else None)
                if not last and 2 <= k < 4:
                    push(b + 1, k % 2)
                if k >= LAG:
                    pop(b, k - LAG)
                elif not first:
                    pop(b - 1, k - LAG + groups)

        push(0, 0)
        push(0, 1)
        block(0, True, False)
        pl.loop(1, NB - 1)(lambda b: block(b, False, False))
        block(NB - 1, False, True)
        for k in range(groups - LAG, groups):
            pop(NB - 1, k)

    def out_copy(slot, k):
        at = pl.ds(pl.multiple_of(place_ref[k] * OWN, OWN), OWN)
        return pltpu.make_async_copy(staged.at[slot], out_ref.at[:, at, :], sems.at[slot])

    offsets = tile_offsets(2 * F)

    def lags_of(half, *accs):
        for g in range(HALF_ROWS // OWN):
            k = half * (HALF_ROWS // OWN) + g

            def pop(u):
                z = pltpu.matmul_pop(accs[u % 8])
                for h in range(2):
                    lagged[h, u * LAG_ROWS : (u + 1) * LAG_ROWS, :] = z[:LAG_ROWS, h * 128 : (h + 1) * 128]

            for u in range(0, OWN, 2):
                for t, at in enumerate(offsets):
                    for v in (u, u + 1):
                        pltpu.matmul_push_rhs(cross[g * OWN + v, at : at + 256, :], t % 2, v % 2)
                    for v in (u, u + 1):
                        pltpu.matmul_acc_lhs(accs[v % 8], table_ref[t], t % 2)
                if u >= 4:
                    pop(u - 4)
                    pop(u - 3)
            for u in range(OWN - 4, OWN):
                pop(u)
            slot = k % 2
            if k >= 2:
                out_copy(slot, k - 2).wait()
            for lag in range(LAGS):
                for h in range(2):
                    v = lagged[h, pl.ds(lag, OWN, stride=LAG_ROWS), :] * (1.0 / math.sqrt(W * F))
                    staged[slot, lag, :, h * 128 : (h + 1) * 128] = v.astype(jnp.bfloat16)
            out_copy(slot, k).start()

    for half in range(n_rows * OWN // HALF_ROWS):
        pl.run_scoped(
            functools.partial(cross_of, half),
            *[pltpu.ACC(mxu)((128, 256), jnp.float32) for mxu in [0] * DEPTH + [1] * DEPTH],
        )
        pl.run_scoped(
            functools.partial(lags_of, half),
            *[pltpu.ACC(mxu)((LAG_TILE, 256), jnp.float32) for mxu in (0, 1) * 4],
        )
    for k in range(n_rows - 2, n_rows):
        out_copy(k % 2, k).wait()


def correlate(places, row_blocks, col_blocks):
    n, m = OWN * len(row_blocks), OWN * len(col_blocks)
    vmem = pl.BlockSpec(memory_space=pltpu.VMEM)
    tables = jnp.asarray(lag_tables(tile_offsets(2 * F)), jnp.bfloat16)
    return pl.pallas_call(
        functools.partial(correlate_kernel, len(row_blocks), len(col_blocks)),
        in_specs=[pl.BlockSpec(memory_space=pltpu.SMEM)] + [vmem] * (len(row_blocks) + len(col_blocks) + 1),
        out_specs=pl.BlockSpec(memory_space=pl.ANY),
        out_shape=jax.ShapeDtypeStruct((LAGS, n, m), jnp.bfloat16),
        scratch_shapes=[
            pltpu.VMEM((m, LANES), jnp.bfloat16),
            pltpu.VMEM((HALF_ROWS, 2 * F, m), jnp.bfloat16),
            pltpu.VMEM((2, OWN * LAG_ROWS, 128), jnp.float32),
            pltpu.VMEM((2, LAGS, OWN, m), jnp.bfloat16),
            pltpu.SemaphoreType.DMA((2,)),
        ],
        compiler_params=pltpu.CompilerParams(vmem_limit_bytes=56 * 1024 * 1024),
    )(places, *row_blocks, *col_blocks, tables)


def gather8(block, move):
    side, before, after = move(block, 0, 1), move(block, 1, 0), move(block, -1, 0)
    found = {(0, 0): block, (0, 1): side, (-1, 0): before, (1, 0): after}
    found[-1, 1] = move(side, 1, 0)
    found[1, 1] = move(side, -1, 0)
    found[2, 0] = move(before, 1, 0)
    found[2, 1] = move(after, -1, 1)
    return found


def body(spectra, offsets, channel_mask):
    white = whiten(spectra, offsets, channel_mask)
    p, src = lax.axis_index("rcv"), lax.axis_index("src")
    q, core = src // 2, src % 2

    def step(index, ring, side):
        return (index ^ (4 * side)) & 4 | (index + ring) & 3

    def over_rcv(value, ring, side):
        return lax.ppermute(value, "rcv", [(i, step(i, ring, side)) for i in range(8)])

    def over_src(value, ring, side):
        return lax.ppermute(value, "src", [(i, 2 * step(i // 2, ring, side) + i % 2) for i in range(16)])

    def other_core(value):
        return lax.ppermute(value, "src", [(i, i ^ 1) for i in range(16)])

    flip = [
        ((i * 2 + k) * 8 + step(j, 2, 0), (j * 2 + k) * 8 + i) for i in range(8) for k in range(2) for j in range(8)
    ]
    turned = lax.ppermute(white, ("src", "rcv"), flip)
    white, turned = lax.optimization_barrier((white, turned))
    rows = gather8(white, over_rcv)
    cols = gather8(turned, over_src)
    swapped = {key: other_core(value) for key, value in cols.items()}
    places = [step(p, *key) for key in rows]
    places += [core * 8 + step(step(q, *key), 2, 0) for key in cols]
    places += [(1 - core) * 8 + step(step(q, *key), 2, 0) for key in swapped]
    places = jnp.stack(places).astype(jnp.int32)
    return correlate(places, list(rows.values()), list(cols.values()) + list(swapped.values()))


def solution(mesh):
    in_specs = (P(("src", "rcv"), None, None, None), P(("src", "rcv"), None), P(("src", "rcv")))
    out_specs = P(None, "src", "rcv")
    return jax.shard_map(body, mesh=mesh, in_specs=in_specs, out_specs=out_specs, check_vma=False)
```

```python
import functools
import math

import jax
import jax.numpy as jnp
import numpy as np
from jax import lax
from jax.experimental import pallas as pl
from jax.experimental.pallas import tpu as pltpu
from jax.sharding import PartitionSpec as P

W = 10
F = 400
KLO = 6
NT = 12000
HALF = 50
LAGS = 2 * HALF + 1
LAG_ROWS = 56
LAG_TILE = 64
UNROLL = 10
FB = 8
NB = F // FB
OWN = 16
MAIN = 16
TILES = NB + -(-NB // 4)
LANES = TILES * 128
DEPTH = 4
LAG = 3


def unit_circle(turns):
    turns = turns - NT * jnp.floor(turns * (1.0 / NT))
    quarter = jnp.floor(turns * (4.0 / NT) + 0.5)
    a = (turns - (NT // 4) * quarter) * (2.0 * math.pi / NT)
    s = a * a
    sin = a + a * s * (-1 / 6 + s * (1 / 120 + s * (-1 / 5040 + s * (1 / 362880))))
    cos = 1.0 + s * (-0.5 + s * (1 / 24 + s * (-1 / 720 + s * (1 / 40320 + s * (-1 / 3628800)))))
    swap = (quarter == 1.0) | (quarter == 3.0)
    c = jnp.where(swap, sin, cos)
    s = jnp.where(swap, cos, sin)
    c = jnp.where((quarter == 1.0) | (quarter == 2.0), -c, c)
    s = jnp.where((quarter == 2.0) | (quarter == 3.0), -s, s)
    return c, s


def whiten_kernel(mask_ref, spectra_ref, offsets_ref, white_ref, parts):
    freq = (KLO + lax.broadcasted_iota(jnp.int32, (W, F), 1)).astype(jnp.float32)
    eye = lax.broadcasted_iota(jnp.int32, (W, W), 0) == lax.broadcasted_iota(jnp.int32, (W, W), 1)
    parts[3] = jnp.zeros((OWN * 32, 128), jnp.float32)
    for ch in range(OWN):
        re = spectra_ref[ch, 0].astype(jnp.float32)
        im = spectra_ref[ch, 1].astype(jnp.float32)
        power = jnp.sum(re * re + im * im, axis=1, keepdims=True) * (1.0 / F)
        scale = lax.rsqrt(power + 1e-06) * mask_ref[ch].astype(jnp.float32)
        row = jnp.broadcast_to(offsets_ref[ch : ch + 1].astype(jnp.float32), (W, W))
        offset = jnp.sum(jnp.where(eye, row, 0.0), axis=1, keepdims=True)
        c, s = unit_circle(offset * freq)
        out = ((re * c + im * s) * scale, (im * c - re * s) * scale)
        for part in range(2):
            for t in range(4):
                n = min(128, F - 128 * t)
                parts[t, ch * 32 + part * 16 : ch * 32 + part * 16 + W, :n] = out[part][:, 128 * t : 128 * t + n]

    chunk = lax.broadcasted_iota(jnp.int32, (OWN, 128), 1) // 8
    for t in range(4):
        pairs = [parts[t, pl.ds(16 * (m % 2) + m // 2, OWN, stride=32), :] for m in range(2 * W)]
        main, rest = pairs[:MAIN], pairs[MAIN:]
        for values, low, bits in ((main, 0, 4), (rest, 2, 2)):
            for bit in range(bits):
                shift = 8 << (low + bit)
                upper = (chunk >> (low + bit)) % 2 == 1
                for m in range(len(values)):
                    if not m >> bit & 1:
                        a, b = values[m], values[m | 1 << bit]
                        values[m] = jnp.where(upper, pltpu.roll(b, shift, 1), a)
                        values[m | 1 << bit] = jnp.where(upper, b, pltpu.roll(a, 128 - shift, 1))
        for k in range(16):
            if 16 * t + k < NB:
                white_ref[:, (16 * t + k) * 128 : (16 * t + k + 1) * 128] = main[k].astype(jnp.bfloat16)
        for k in range(4):
            tile = NB + 4 * t + k
            if tile < TILES:
                white_ref[:, tile * 128 : (tile + 1) * 128] = rest[k].astype(jnp.bfloat16)


def whiten(spectra, offsets, channel_mask):
    return pl.pallas_call(
        whiten_kernel,
        in_specs=[
            pl.BlockSpec(memory_space=pltpu.SMEM),
            pl.BlockSpec(memory_space=pltpu.VMEM),
            pl.BlockSpec(memory_space=pltpu.VMEM),
        ],
        out_specs=pl.BlockSpec(memory_space=pltpu.VMEM),
        out_shape=jax.ShapeDtypeStruct((OWN, LANES), jnp.bfloat16),
        scratch_shapes=[pltpu.VMEM((4, OWN * 32, 128), jnp.float32)],
    )(channel_mask, spectra, offsets)


def segments():
    return [(t, u) for t in range(OWN * F // 256) for u in range(256 * t // F, (256 * t + 255) // F + 1)]


def lag_tables():
    freq = KLO + np.arange(F)
    angle = 2.0 * math.pi / NT * ((np.arange(HALF + 1)[:, None] * freq[None, :]) % NT)
    tables = np.pad(np.stack([np.cos(angle), -np.sin(angle)]), ((0, 0), (0, LAG_TILE - HALF - 1), (256, 256)))
    return np.stack([tables[:, :, 256 + 256 * t - F * u :][:, :, :256] for t, u in segments()], 1)


def step(index, ring, side):
    return (index ^ (4 * side)) & 4 | (index + ring) & 3


def correlate_kernel(row_keys, col_keys, n_kept, *refs):
    n_rows, n_cols = len(row_keys), 2 * len(col_keys)
    p, q, core = lax.axis_index("rcv"), lax.axis_index("src") // 2, lax.axis_index("src") % 2
    row_places = [step(p, *key) for key in row_keys]
    col_places = [c * 8 + step(step(q, *key), 2, 0) for c in (core, 1 - core) for key in col_keys]
    row_refs, refs = refs[:n_rows], refs[n_rows:]
    col_refs, refs = refs[:n_cols], refs[n_cols:]
    table_ref, out_ref, cols, rows, turned, cross, *lagged, staged, sems = refs[:1] + refs[1 + n_kept :]
    lane = lax.broadcasted_iota(jnp.int32, (16, 128), 1)
    same_bin = (lane % 8) == lax.broadcasted_iota(jnp.int32, (16, 128), 0) % 8
    zero = jnp.zeros((), jnp.bfloat16)
    groups = n_rows * OWN // 8

    for k, ref in enumerate(col_refs):
        cols[pl.ds(pl.multiple_of(col_places[k] * OWN, OWN), OWN), :] = ref[...]

    def spread(first, last, shift):
        minus = (lax.broadcasted_iota(jnp.int32, (OWN, 128), 1) // shift) % 2 == 1

        @pl.loop(first, last, unroll=UNROLL)
        def _(t):
            at = pl.ds(pl.multiple_of(t * 128, 128), 128)
            for k, ref in enumerate(row_refs):
                v = ref[:, at].astype(jnp.float32)
                rows[k * OWN : (k + 1) * OWN, at] = v
                v = jnp.where(minus, -pltpu.roll(v, shift, 1), pltpu.roll(v, 128 - shift, 1))
                turned[k * OWN : (k + 1) * OWN, at] = v

    spread(0, NB, 8)
    spread(NB, TILES, 32)

    def cross_of(*accs):
        accs = accs[:DEPTH], accs[DEPTH:]

        def main_lanes(b):
            return pl.ds(pl.multiple_of(b * 128, 128), 128)

        def rest_lanes(pair):
            return pl.ds(pl.multiple_of((NB + pair // 2) * 128, 128), 128)

        def push(pair):
            for mxu in range(2):
                right = jnp.concatenate([cols[:, main_lanes(2 * pair + mxu)], cols[:, rest_lanes(pair)]], 1)
                pltpu.matmul_push_rhs(right, 0, mxu, transpose=True)

        def wide(i, lanes):
            both = [jnp.broadcast_to(ref[i : i + 1, lanes], (8, 128)) for ref in (rows, turned)]
            return jnp.concatenate(both, 0).astype(jnp.bfloat16)

        def start(pair, k, same_rest):
            left = [], []
            for u in range(8):
                r = wide(8 * k + u, rest_lanes(pair))
                for mxu in range(2):
                    m = wide(8 * k + u, main_lanes(2 * pair + mxu))
                    m, q = jnp.where(same_bin, m, zero), jnp.where(same_rest[mxu], r, zero)
                    left[mxu].append(jnp.concatenate([m, q], 1))
            for mxu in range(2):
                left_rows = jnp.concatenate(left[mxu], 0)
                pltpu.matmul_acc_lhs(accs[mxu][k % DEPTH], left_rows, 0 if k == 0 else None)

        def finish(pair, k):
            product = [pltpu.matmul_pop(accs[mxu][k % DEPTH]) for mxu in range(2)]
            for part in range(2):
                for u in range(8):
                    o = u * 16 + part * 8
                    both = jnp.concatenate([p[o : o + 8] for p in product], 0)
                    at = pl.ds(pl.multiple_of((8 * k + u) * F + pair * 16, 16), 16)
                    cross[part, at, :] = both.astype(jnp.bfloat16)

        def work(pair, first, last):
            same_rest = [same_bin & ((lane // 8) % 4 == (2 * pair + mxu) % 4) for mxu in range(2)]
            for k in range(groups):
                start(pair, k, same_rest)
                if not last and k == 1:
                    push(pair + 1)
                if k >= LAG:
                    finish(pair, k - LAG)
                elif not first:
                    finish(pair - 1, k - LAG + groups)

        push(0)
        work(0, True, False)
        pl.loop(1, NB // 2 - 1)(lambda pair: work(pair, False, False))
        work(NB // 2 - 1, False, True)
        for k in range(groups - LAG, groups):
            finish(NB // 2 - 1, k)

    def out_copy(k):
        at = pl.ds(pl.multiple_of(row_places[k] * OWN, OWN), OWN)
        return pltpu.make_async_copy(staged.at[k % 2], out_ref.at[:, at, :], sems.at[k % 2])

    def emit(g):
        if g >= 2:
            out_copy(g - 2).wait()
        for lag in range(HALF + 1):
            for h in range(2):
                e, o = (lagged[2 * (g % 2) + part][h, pl.ds(lag, OWN, stride=LAG_ROWS), :] for part in range(2))
                lanes = slice(h * 128, (h + 1) * 128)
                staged[g % 2, HALF + lag, :, lanes] = ((e + o) * (1.0 / math.sqrt(W * F))).astype(jnp.bfloat16)
                if lag:
                    staged[g % 2, HALF - lag, :, lanes] = ((e - o) * (1.0 / math.sqrt(W * F))).astype(jnp.bfloat16)
        out_copy(g).start()

    def lags_of(*accs):
        accs = accs[:4], accs[4:]

        def push(g, t):
            at = g * OWN * F + t * 256
            for part in range(2):
                pltpu.matmul_push_rhs(cross[part, at : at + 256, :], t % 2, part)

        def finish(g, u):
            for part in range(2):
                z = pltpu.matmul_pop(accs[part][u % 4])
                for h in range(2):
                    rows_of = slice(u * LAG_ROWS, (u + 1) * LAG_ROWS)
                    lagged[2 * (g % 2) + part][h, rows_of, :] = z[:LAG_ROWS, h * 128 : (h + 1) * 128]

        for g in range(n_rows):
            pushed = done = -1
            for k, (t, u) in enumerate(segments()):
                if t != pushed:
                    push(g, t)
                for part in range(2):
                    pltpu.matmul_acc_lhs(accs[part][u % 4], table_ref[part, k], t % 2 if t != pushed else None)
                pushed = t
                if u - 2 > done:
                    done = u - 2
                    finish(g, done)
            for u in range(done + 1, OWN):
                finish(g, u)
            if g:
                emit(g - 1)
        emit(n_rows - 1)

    pl.run_scoped(cross_of, *[pltpu.ACC(mxu)((128, 256), jnp.float32) for mxu in [0] * DEPTH + [1] * DEPTH])
    pl.run_scoped(lags_of, *[pltpu.ACC(mxu)((LAG_TILE, 256), jnp.float32) for mxu in [0] * 4 + [1] * 4])
    for k in range(n_rows - 2, n_rows):
        out_copy(k).wait()


def correlate(rows, cols, swapped, shape, kept=()):
    row_blocks, col_blocks = list(rows.values()), list(cols.values()) + [swapped[key] for key in cols]
    n, m = OWN * len(row_blocks), OWN * len(col_blocks)
    vmem, anywhere = pl.BlockSpec(memory_space=pltpu.VMEM), pl.BlockSpec(memory_space=pl.ANY)
    inputs = (*row_blocks, *col_blocks, jnp.asarray(lag_tables(), jnp.bfloat16), *kept)
    return pl.pallas_call(
        functools.partial(correlate_kernel, tuple(rows), tuple(cols), len(kept)),
        in_specs=[vmem] * (len(row_blocks) + len(col_blocks) + 1) + [anywhere] * len(kept),
        out_specs=anywhere,
        out_shape=jax.ShapeDtypeStruct(shape, jnp.bfloat16),
        input_output_aliases={len(inputs) - 1: 0} if kept else {},
        scratch_shapes=[
            pltpu.VMEM((m, LANES), jnp.bfloat16),
            pltpu.VMEM((n, LANES), jnp.float32),
            pltpu.VMEM((n, LANES), jnp.float32),
            pltpu.VMEM((2, n * F, m), jnp.bfloat16),
            *[pltpu.VMEM((2, OWN * LAG_ROWS, 128), jnp.float32)] * 4,
            pltpu.VMEM((2, LAGS, OWN, m), jnp.bfloat16),
            pltpu.SemaphoreType.DMA((2,)),
        ],
        compiler_params=pltpu.CompilerParams(vmem_limit_bytes=52 * 1024 * 1024),
        cost_estimate=pl.CostEstimate(flops=n * 2 * 10**8, bytes_accessed=10**7, transcendentals=0),
    )(*inputs)


def near(block, move):
    return {(0, 0): block, (0, 1): move(block, 0, 1), (-1, 0): move(block, 1, 0), (1, 0): move(block, -1, 0)}


def far(found, move):
    return {
        (-1, 1): move(found[0, 1], 1, 0),
        (1, 1): move(found[0, 1], -1, 0),
        (2, 0): move(found[-1, 0], 1, 0),
        (2, 1): move(found[1, 0], -1, 1),
    }


def body(spectra, offsets, channel_mask):
    white = whiten(spectra, offsets, channel_mask)

    def over_rcv(value, ring, side):
        return lax.ppermute(value, "rcv", [(i, step(i, ring, side)) for i in range(8)])

    def over_src(value, ring, side):
        return lax.ppermute(value, "src", [(i, 2 * step(i // 2, ring, side) + i % 2) for i in range(16)])

    def other_core(value):
        return lax.ppermute(value, "src", [(i, i ^ 1) for i in range(16)])

    flip = [
        ((i * 2 + k) * 8 + step(j, 2, 0), (j * 2 + k) * 8 + i) for i in range(8) for k in range(2) for j in range(8)
    ]
    turned = lax.ppermute(white, ("src", "rcv"), flip)
    cols = near(turned, over_src)
    swapped = {(0, 0): other_core(turned)}
    white, swapped[0, 0] = lax.optimization_barrier((white, swapped[0, 0]))
    rows = near(white, over_rcv)
    more = far(cols, over_src)
    swapped |= {key: other_core(value) for key, value in (cols | more).items() if key != (0, 0)}
    cols |= more
    rows, swapped = lax.optimization_barrier((rows, swapped))
    shape = (LAGS, 8 * OWN, 16 * OWN)
    first = correlate(rows, cols, swapped, shape)
    return correlate(far(rows, over_rcv), cols, swapped, shape, (first,))


def solution(mesh):
    in_specs = (P(("src", "rcv"), None, None, None), P(("src", "rcv"), None), P(("src", "rcv")))
    out_specs = P(None, "src", "rcv")
    return jax.shard_map(body, mesh=mesh, in_specs=in_specs, out_specs=out_specs, check_vma=False)
```

```python
import functools
import math

import jax
import jax.numpy as jnp
import numpy as np
from jax import lax
from jax.experimental import pallas as pl
from jax.experimental.pallas import tpu as pltpu
from jax.sharding import PartitionSpec as P

W = 10
F = 400
KLO = 6
NT = 12000
HALF = 50
LAGS = 2 * HALF + 1
LAG_ROWS = 56
LAG_TILE = 64
UNROLL = 10
FB = 8
NB = F // FB
OWN = 16
MAIN = 16
TILES = NB + -(-NB // 4)
LANES = TILES * 128
DEPTH = 4
LAG = 3


def unit_circle(turns):
    turns = turns - NT * jnp.floor(turns * (1.0 / NT))
    quarter = jnp.floor(turns * (4.0 / NT) + 0.5)
    a = (turns - (NT // 4) * quarter) * (2.0 * math.pi / NT)
    s = a * a
    sin = a + a * s * (-1 / 6 + s * (1 / 120 + s * (-1 / 5040 + s * (1 / 362880))))
    cos = 1.0 + s * (-0.5 + s * (1 / 24 + s * (-1 / 720 + s * (1 / 40320 + s * (-1 / 3628800)))))
    swap = (quarter == 1.0) | (quarter == 3.0)
    c = jnp.where(swap, sin, cos)
    s = jnp.where(swap, cos, sin)
    c = jnp.where((quarter == 1.0) | (quarter == 2.0), -c, c)
    s = jnp.where((quarter == 2.0) | (quarter == 3.0), -s, s)
    return c, s


def whiten_kernel(mask_ref, spectra_ref, offsets_ref, white_ref, parts):
    freq = (KLO + lax.broadcasted_iota(jnp.int32, (W, F), 1)).astype(jnp.float32)
    eye = lax.broadcasted_iota(jnp.int32, (W, W), 0) == lax.broadcasted_iota(jnp.int32, (W, W), 1)
    parts[3] = jnp.zeros((OWN * 32, 128), jnp.float32)
    for ch in range(OWN):
        re = spectra_ref[ch, 0].astype(jnp.float32)
        im = spectra_ref[ch, 1].astype(jnp.float32)
        power = jnp.sum(re * re + im * im, axis=1, keepdims=True) * (1.0 / F)
        scale = lax.rsqrt(power + 1e-06) * mask_ref[ch].astype(jnp.float32)
        row = jnp.broadcast_to(offsets_ref[ch : ch + 1].astype(jnp.float32), (W, W))
        offset = jnp.sum(jnp.where(eye, row, 0.0), axis=1, keepdims=True)
        c, s = unit_circle(offset * freq)
        out = ((re * c + im * s) * scale, (im * c - re * s) * scale)
        for part in range(2):
            for t in range(4):
                n = min(128, F - 128 * t)
                parts[t, ch * 32 + part * 16 : ch * 32 + part * 16 + W, :n] = out[part][:, 128 * t : 128 * t + n]

    chunk = lax.broadcasted_iota(jnp.int32, (OWN, 128), 1) // 8
    for t in range(4):
        pairs = [parts[t, pl.ds(16 * (m % 2) + m // 2, OWN, stride=32), :] for m in range(2 * W)]
        main, rest = pairs[:MAIN], pairs[MAIN:]
        for values, low, bits in ((main, 0, 4), (rest, 2, 2)):
            for bit in range(bits):
                shift = 8 << (low + bit)
                upper = (chunk >> (low + bit)) % 2 == 1
                for m in range(len(values)):
                    if not m >> bit & 1:
                        a, b = values[m], values[m | 1 << bit]
                        values[m] = jnp.where(upper, pltpu.roll(b, shift, 1), a)
                        values[m | 1 << bit] = jnp.where(upper, b, pltpu.roll(a, 128 - shift, 1))
        for k in range(16):
            if 16 * t + k < NB:
                white_ref[:, (16 * t + k) * 128 : (16 * t + k + 1) * 128] = main[k].astype(jnp.bfloat16)
        for k in range(4):
            tile = NB + 4 * t + k
            if tile < TILES:
                white_ref[:, tile * 128 : (tile + 1) * 128] = rest[k].astype(jnp.bfloat16)


def whiten(spectra, offsets, channel_mask):
    return pl.pallas_call(
        whiten_kernel,
        in_specs=[
            pl.BlockSpec(memory_space=pltpu.SMEM),
            pl.BlockSpec(memory_space=pltpu.VMEM),
            pl.BlockSpec(memory_space=pltpu.VMEM),
        ],
        out_specs=pl.BlockSpec(memory_space=pltpu.VMEM),
        out_shape=jax.ShapeDtypeStruct((OWN, LANES), jnp.bfloat16),
        scratch_shapes=[pltpu.VMEM((4, OWN * 32, 128), jnp.float32)],
    )(channel_mask, spectra, offsets)


def segments():
    return [(t, u) for t in range(OWN * F // 256) for u in range(256 * t // F, (256 * t + 255) // F + 1)]


def lag_tables():
    freq = KLO + np.arange(F)
    angle = 2.0 * math.pi / NT * ((np.arange(HALF + 1)[:, None] * freq[None, :]) % NT)
    tables = np.pad(np.stack([np.cos(angle), -np.sin(angle)]), ((0, 0), (0, LAG_TILE - HALF - 1), (256, 256)))
    return np.stack([tables[:, :, 256 + 256 * t - F * u :][:, :, :256] for t, u in segments()], 1)


def step(index, ring, side):
    return (index ^ (4 * side)) & 4 | (index + ring) & 3


def correlate_kernel(row_keys, col_keys, n_kept, *refs):
    n_rows, n_cols = len(row_keys), 2 * len(col_keys)
    p, q, core = lax.axis_index("rcv"), lax.axis_index("src") // 2, lax.axis_index("src") % 2
    row_places = [step(p, *key) for key in row_keys]
    row_refs, refs = refs[:n_rows], refs[n_rows:]
    col_refs, refs = refs[:n_cols], refs[n_cols:]
    table_from, out_ref, cols, table_ref, rows, turned, cross, *lagged, staged, sems, in_sems = (
        refs[:1] + refs[1 + n_kept :]
    )
    lane = lax.broadcasted_iota(jnp.int32, (16, 128), 1)
    same_bin = (lane % 8) == lax.broadcasted_iota(jnp.int32, (16, 128), 0) % 8
    zero = jnp.zeros((), jnp.bfloat16)
    groups = n_rows * OWN // 8

    loads = [pltpu.make_async_copy(table_from, table_ref, in_sems.at[4 * n_cols])]
    for k, ref in enumerate(col_refs):
        c = core if k < n_cols // 2 else 1 - core
        for u, key in enumerate(col_keys[k % len(col_keys)]):
            at = pl.ds(pl.multiple_of((c * 8 + step(step(q, *key), 2, 0)) * OWN, OWN), OWN)
            piece = ref.at[u * OWN : (u + 1) * OWN, :]
            loads.append(pltpu.make_async_copy(piece, cols.at[at, :], in_sems.at[4 * k + u]))
    for load in loads[1:] + loads[:1]:
        load.start()

    def spread(first, last, shift):
        minus = (lax.broadcasted_iota(jnp.int32, (OWN, 128), 1) // shift) % 2 == 1

        @pl.loop(first, last, unroll=UNROLL)
        def _(t):
            at = pl.ds(pl.multiple_of(t * 128, 128), 128)
            for k, ref in enumerate(row_refs):
                v = ref[:, at].astype(jnp.float32)
                rows[k * OWN : (k + 1) * OWN, at] = v
                v = jnp.where(minus, -pltpu.roll(v, shift, 1), pltpu.roll(v, 128 - shift, 1))
                turned[k * OWN : (k + 1) * OWN, at] = v

    spread(0, NB, 8)
    spread(NB, TILES, 32)
    for load in loads[1:]:
        load.wait()

    def cross_of(*accs):
        accs = accs[:DEPTH], accs[DEPTH:]

        def main_lanes(b):
            return pl.ds(pl.multiple_of(b * 128, 128), 128)

        def rest_lanes(pair):
            return pl.ds(pl.multiple_of((NB + pair // 2) * 128, 128), 128)

        def push(pair):
            for mxu in range(2):
                right = jnp.concatenate([cols[:, main_lanes(2 * pair + mxu)], cols[:, rest_lanes(pair)]], 1)
                pltpu.matmul_push_rhs(right, 0, mxu, transpose=True)

        def wide(i, lanes):
            both = [jnp.broadcast_to(ref[i : i + 1, lanes], (8, 128)) for ref in (rows, turned)]
            return jnp.concatenate(both, 0).astype(jnp.bfloat16)

        def start(pair, k, same_rest):
            left = [], []
            for u in range(8):
                r = wide(8 * k + u, rest_lanes(pair))
                for mxu in range(2):
                    m = wide(8 * k + u, main_lanes(2 * pair + mxu))
                    m, q = jnp.where(same_bin, m, zero), jnp.where(same_rest[mxu], r, zero)
                    left[mxu].append(jnp.concatenate([m, q], 1))
            for mxu in range(2):
                left_rows = jnp.concatenate(left[mxu], 0)
                pltpu.matmul_acc_lhs(accs[mxu][k % DEPTH], left_rows, 0 if k == 0 else None)

        def finish(pair, k):
            product = [pltpu.matmul_pop(accs[mxu][k % DEPTH]) for mxu in range(2)]
            for part in range(2):
                for u in range(8):
                    o = u * 16 + part * 8
                    both = jnp.concatenate([p[o : o + 8] for p in product], 0)
                    at = pl.ds(pl.multiple_of((8 * k + u) * F + pair * 16, 16), 16)
                    cross[part, at, :] = both.astype(jnp.bfloat16)

        def work(pair, first, last):
            same_rest = [same_bin & ((lane // 8) % 4 == (2 * pair + mxu) % 4) for mxu in range(2)]
            for k in range(groups):
                start(pair, k, same_rest)
                if not last and k == 1:
                    push(pair + 1)
                if k >= LAG:
                    finish(pair, k - LAG)
                elif not first:
                    finish(pair - 1, k - LAG + groups)

        push(0)
        work(0, True, False)
        pl.loop(1, NB // 2 - 1)(lambda pair: work(pair, False, False))
        work(NB // 2 - 1, False, True)
        for k in range(groups - LAG, groups):
            finish(NB // 2 - 1, k)

    def out_copy(k):
        at = pl.ds(pl.multiple_of(row_places[k] * OWN, OWN), OWN)
        return pltpu.make_async_copy(staged.at[k % 2], out_ref.at[:, at, :], sems.at[k % 2])

    def emit(g):
        if g >= 2:
            out_copy(g - 2).wait()
        for lag in range(HALF + 1):
            for h in range(2):
                e, o = (lagged[2 * (g % 2) + part][h, pl.ds(lag, OWN, stride=LAG_ROWS), :] for part in range(2))
                lanes = slice(h * 128, (h + 1) * 128)
                staged[g % 2, HALF + lag, :, lanes] = ((e + o) * (1.0 / math.sqrt(W * F))).astype(jnp.bfloat16)
                if lag:
                    staged[g % 2, HALF - lag, :, lanes] = ((e - o) * (1.0 / math.sqrt(W * F))).astype(jnp.bfloat16)
        out_copy(g).start()

    def lags_of(*accs):
        accs = accs[:4], accs[4:]

        def push(g, t):
            at = g * OWN * F + t * 256
            for part in range(2):
                pltpu.matmul_push_rhs(cross[part, at : at + 256, :], t % 2, part)

        def finish(g, u):
            for part in range(2):
                z = pltpu.matmul_pop(accs[part][u % 4])
                for h in range(2):
                    rows_of = slice(u * LAG_ROWS, (u + 1) * LAG_ROWS)
                    lagged[2 * (g % 2) + part][h, rows_of, :] = z[:LAG_ROWS, h * 128 : (h + 1) * 128]

        for g in range(n_rows):
            pushed = done = -1
            for k, (t, u) in enumerate(segments()):
                if t != pushed:
                    push(g, t)
                for part in range(2):
                    pltpu.matmul_acc_lhs(accs[part][u % 4], table_ref[part, k], t % 2 if t != pushed else None)
                pushed = t
                if u - 2 > done:
                    done = u - 2
                    finish(g, done)
            for u in range(done + 1, OWN):
                finish(g, u)
            if g:
                emit(g - 1)
        emit(n_rows - 1)

    pl.run_scoped(cross_of, *[pltpu.ACC(mxu)((128, 256), jnp.float32) for mxu in [0] * DEPTH + [1] * DEPTH])
    loads[0].wait()
    pl.run_scoped(lags_of, *[pltpu.ACC(mxu)((LAG_TILE, 256), jnp.float32) for mxu in [0] * 4 + [1] * 4])
    for k in range(n_rows - 2, n_rows):
        out_copy(k).wait()


def correlate(rows, cols, swapped, shape, kept=()):
    row_blocks, col_blocks = list(rows.values()), list(cols.values()) + [swapped[keys] for keys in cols]
    n, m = OWN * len(row_blocks), 4 * OWN * len(col_blocks)
    vmem, anywhere = pl.BlockSpec(memory_space=pltpu.VMEM), pl.BlockSpec(memory_space=pl.ANY)
    inputs = (*row_blocks, *col_blocks, jnp.asarray(lag_tables(), jnp.bfloat16), *kept)
    return pl.pallas_call(
        functools.partial(correlate_kernel, tuple(rows), tuple(cols), len(kept)),
        in_specs=[vmem] * len(row_blocks) + [anywhere] * (len(col_blocks) + 1 + len(kept)),
        out_specs=anywhere,
        out_shape=jax.ShapeDtypeStruct(shape, jnp.bfloat16),
        input_output_aliases={len(inputs) - 1: 0} if kept else {},
        scratch_shapes=[
            pltpu.VMEM((m, LANES), jnp.bfloat16),
            pltpu.VMEM((2, len(segments()), LAG_TILE, 256), jnp.bfloat16),
            pltpu.VMEM((n, LANES), jnp.float32),
            pltpu.VMEM((n, LANES), jnp.float32),
            pltpu.VMEM((2, n * F, m), jnp.bfloat16),
            *[pltpu.VMEM((2, OWN * LAG_ROWS, 128), jnp.float32)] * 4,
            pltpu.VMEM((2, LAGS, OWN, m), jnp.bfloat16),
            pltpu.SemaphoreType.DMA((2,)),
            pltpu.SemaphoreType.DMA((4 * len(col_blocks) + 1,)),
        ],
        compiler_params=pltpu.CompilerParams(vmem_limit_bytes=54 * 1024 * 1024),
        cost_estimate=pl.CostEstimate(flops=n * 2 * 10**8, bytes_accessed=10**7, transcendentals=0),
    )(*inputs)


def body(spectra, offsets, channel_mask):
    white = whiten(spectra, offsets, channel_mask)

    def over_rcv(value, ring, side):
        return lax.ppermute(value, "rcv", [(i, step(i, ring, side)) for i in range(8)])

    def over_src(value, ring, side):
        return lax.ppermute(value, "src", [(i, 2 * step(i // 2, ring, side) + i % 2) for i in range(16)])

    def other_core(value):
        return lax.ppermute(value, "src", [(i, i ^ 1) for i in range(16)])

    flip = [
        ((i * 2 + k) * 8 + step(j, 2, 0), (j * 2 + k) * 8 + i) for i in range(8) for k in range(2) for j in range(8)
    ]
    turned = lax.ppermute(white, ("src", "rcv"), flip)
    side, turned = lax.optimization_barrier((over_rcv(white, 0, 1), turned))
    rows = {(0, 0): white, (0, 1): side}

    cols = {(0, 0): turned}
    for key in ((-1, 0), (1, 0), (0, 1), (-1, 1), (1, 1)):
        cols[key] = over_src(turned, -key[0], key[1])
    cols[2, 0] = over_src(cols[-1, 0], 1, 0)
    cols[2, 1] = over_src(cols[1, 1], -1, 0)
    pieces = ((0, 0), (-1, 0), (1, 0), (0, 1)), ((-1, 1), (1, 1), (2, 0), (2, 1))
    cols = {keys: jnp.concatenate([cols[key] for key in keys], 0) for keys in pieces}
    swapped = {keys: other_core(value) for keys, value in cols.items()}

    white, cols[pieces[0]] = lax.optimization_barrier((white, cols[pieces[0]]))
    rows[-1, 0], rows[1, 0] = over_rcv(white, 1, 0), over_rcv(white, -1, 0)
    side, before, after, swapped[pieces[0]] = lax.optimization_barrier((side, rows[-1, 0], rows[1, 0], swapped[pieces[0]]))
    late = {
        (-1, 1): over_rcv(side, 1, 0),
        (1, 1): over_rcv(side, -1, 0),
        (2, 0): over_rcv(before, 1, 0),
        (2, 1): over_rcv(after, -1, 1),
    }
    shape = (LAGS, 8 * OWN, 16 * OWN)
    first = correlate(rows, cols, swapped, shape)
    return correlate(late, cols, swapped, shape, (first,))


def solution(mesh):
    in_specs = (P(("src", "rcv"), None, None, None), P(("src", "rcv"), None), P(("src", "rcv")))
    out_specs = P(None, "src", "rcv")
    return jax.shard_map(body, mesh=mesh, in_specs=in_specs, out_specs=out_specs, check_vma=False)
```

```python
import functools
import math

import jax
import jax.numpy as jnp
import numpy as np
from jax import lax
from jax.experimental import pallas as pl
from jax.experimental.pallas import tpu as pltpu
from jax.sharding import PartitionSpec as P

W = 10
F = 400
KLO = 6
NT = 12000
HALF = 50
LAGS = 2 * HALF + 1
LAG_ROWS = 56
LAG_TILE = 64
UNROLL = 10
TOGETHER = 2
FB = 8
NB = F // FB
OWN = 16
MAIN = 16
TILES = NB + -(-NB // 4)
LANES = TILES * 128
DEPTH = 8
LAG = 4


def unit_circle(turns):
    turns = turns - NT * jnp.floor(turns * (1.0 / NT))
    quarter = jnp.floor(turns * (4.0 / NT) + 0.5)
    a = (turns - (NT // 4) * quarter) * (2.0 * math.pi / NT)
    s = a * a
    sin = a + a * s * (-1 / 6 + s * (1 / 120 + s * (-1 / 5040 + s * (1 / 362880))))
    cos = 1.0 + s * (-0.5 + s * (1 / 24 + s * (-1 / 720 + s * (1 / 40320 + s * (-1 / 3628800)))))
    swap = (quarter == 1.0) | (quarter == 3.0)
    c = jnp.where(swap, sin, cos)
    s = jnp.where(swap, cos, sin)
    c = jnp.where((quarter == 1.0) | (quarter == 2.0), -c, c)
    s = jnp.where((quarter == 2.0) | (quarter == 3.0), -s, s)
    return c, s


def whiten_kernel(mask_ref, spectra_ref, offsets_ref, white_ref, parts):
    freq = (KLO + lax.broadcasted_iota(jnp.int32, (W, F), 1)).astype(jnp.float32)
    eye = lax.broadcasted_iota(jnp.int32, (W, W), 0) == lax.broadcasted_iota(jnp.int32, (W, W), 1)
    parts[3] = jnp.zeros((OWN * 32, 128), jnp.float32)
    for ch in range(OWN):
        re = spectra_ref[ch, 0].astype(jnp.float32)
        im = spectra_ref[ch, 1].astype(jnp.float32)
        power = jnp.sum(re * re + im * im, axis=1, keepdims=True) * (1.0 / F)
        scale = lax.rsqrt(power + 1e-06) * mask_ref[ch].astype(jnp.float32)
        row = jnp.broadcast_to(offsets_ref[ch : ch + 1].astype(jnp.float32), (W, W))
        offset = jnp.sum(jnp.where(eye, row, 0.0), axis=1, keepdims=True)
        c, s = unit_circle(offset * freq)
        out = ((re * c + im * s) * scale, (im * c - re * s) * scale)
        for part in range(2):
            for t in range(4):
                n = min(128, F - 128 * t)
                parts[t, ch * 32 + part * 16 : ch * 32 + part * 16 + W, :n] = out[part][:, 128 * t : 128 * t + n]

    chunk = lax.broadcasted_iota(jnp.int32, (OWN, 128), 1) // 8
    for t in range(4):
        pairs = [parts[t, pl.ds(16 * (m % 2) + m // 2, OWN, stride=32), :] for m in range(2 * W)]
        main, rest = pairs[:MAIN], pairs[MAIN:]
        for values, low, bits in ((main, 0, 4), (rest, 2, 2)):
            for bit in range(bits):
                shift = 8 << (low + bit)
                upper = (chunk >> (low + bit)) % 2 == 1
                for m in range(len(values)):
                    if not m >> bit & 1:
                        a, b = values[m], values[m | 1 << bit]
                        values[m] = jnp.where(upper, pltpu.roll(b, shift, 1), a)
                        values[m | 1 << bit] = jnp.where(upper, b, pltpu.roll(a, 128 - shift, 1))
        for k in range(16):
            if 16 * t + k < NB:
                white_ref[:, (16 * t + k) * 128 : (16 * t + k + 1) * 128] = main[k].astype(jnp.bfloat16)
        for k in range(4):
            tile = NB + 4 * t + k
            if tile < TILES:
                white_ref[:, tile * 128 : (tile + 1) * 128] = rest[k].astype(jnp.bfloat16)


def whiten(spectra, offsets, channel_mask):
    return pl.pallas_call(
        whiten_kernel,
        in_specs=[
            pl.BlockSpec(memory_space=pltpu.SMEM),
            pl.BlockSpec(memory_space=pltpu.VMEM),
            pl.BlockSpec(memory_space=pltpu.VMEM),
        ],
        out_specs=pl.BlockSpec(memory_space=pltpu.VMEM),
        out_shape=jax.ShapeDtypeStruct((OWN, LANES), jnp.bfloat16),
        scratch_shapes=[pltpu.VMEM((4, OWN * 32, 128), jnp.float32)],
    )(channel_mask, spectra, offsets)


def segments():
    return [(t, u) for t in range(OWN * F // 256) for u in range(256 * t // F, (256 * t + 255) // F + 1)]


def lag_tables():
    freq = KLO + np.arange(F)
    angle = 2.0 * math.pi / NT * ((np.arange(HALF + 1)[:, None] * freq[None, :]) % NT)
    tables = np.pad(np.stack([np.cos(angle), -np.sin(angle)]), ((0, 0), (0, LAG_TILE - HALF - 1), (256, 256)))
    return np.stack([tables[:, :, 256 + 256 * t - F * u :][:, :, :256] for t, u in segments()], 1)


def step(index, ring, side):
    return (index ^ (4 * side)) & 4 | (index + ring) & 3


def correlate_kernel(row_keys, col_keys, n_kept, *refs):
    n_rows, n_cols = len(row_keys), 2 * len(col_keys)
    p, q, core = lax.axis_index("rcv"), lax.axis_index("src") // 2, lax.axis_index("src") % 2
    row_places = [step(p, *key) for key in row_keys]
    col_places = [c * 8 + step(step(q, *key), 2, 0) for c in (core, 1 - core) for key in col_keys]
    row_refs, refs = refs[:n_rows], refs[n_rows:]
    col_refs, refs = refs[:n_cols], refs[n_cols:]
    table_from, out_ref, cols, table_ref, rows, turned, cross, *lagged, staged, sems, in_sems = (
        refs[:1] + refs[1 + n_kept :]
    )
    lane = lax.broadcasted_iota(jnp.int32, (16, 128), 1)
    same_bin = (lane % 8) == lax.broadcasted_iota(jnp.int32, (16, 128), 0) % 8
    zero = jnp.zeros((), jnp.bfloat16)
    groups = n_rows * OWN // 8

    loads = []
    for k, ref in enumerate(col_refs):
        at = pl.ds(pl.multiple_of(col_places[k] * OWN, OWN), OWN)
        loads.append(pltpu.make_async_copy(ref, cols.at[at, :], in_sems.at[k]))
    loads.append(pltpu.make_async_copy(table_from, table_ref, in_sems.at[n_cols]))
    for load in loads:
        load.start()

    def spread(first, last, shift):
        minus = (lax.broadcasted_iota(jnp.int32, (OWN, 128), 1) // shift) % 2 == 1

        @pl.loop(first, last, unroll=UNROLL)
        def _(t):
            at = pl.ds(pl.multiple_of(t * 128, 128), 128)
            for k, ref in enumerate(row_refs):
                v = ref[:, at].astype(jnp.float32)
                rows[k * OWN : (k + 1) * OWN, at] = v
                v = jnp.where(minus, -pltpu.roll(v, shift, 1), pltpu.roll(v, 128 - shift, 1))
                turned[k * OWN : (k + 1) * OWN, at] = v

    spread(0, NB, 8)
    spread(NB, TILES, 32)
    for load in loads[:-1]:
        load.wait()

    def cross_of(*accs):
        accs = accs[:DEPTH], accs[DEPTH:]

        def main_lanes(b):
            return pl.ds(pl.multiple_of(b * 128, 128), 128)

        def rest_lanes(pair):
            return pl.ds(pl.multiple_of((NB + pair // 2) * 128, 128), 128)

        def push(pair):
            for mxu in range(2):
                right = jnp.concatenate([cols[:, main_lanes(2 * pair + mxu)], cols[:, rest_lanes(pair)]], 1)
                pltpu.matmul_push_rhs(right, 0, mxu, transpose=True)

        def wide(i, lanes):
            both = [jnp.broadcast_to(ref[i : i + 1, lanes], (8, 128)) for ref in (rows, turned)]
            return jnp.concatenate(both, 0).astype(jnp.bfloat16)

        def start(pair, k, same_rest):
            left = [], []
            for u in range(8):
                r = wide(8 * k + u, rest_lanes(pair))
                for mxu in range(2):
                    m = wide(8 * k + u, main_lanes(2 * pair + mxu))
                    m, q = jnp.where(same_bin, m, zero), jnp.where(same_rest[mxu], r, zero)
                    left[mxu].append(jnp.concatenate([m, q], 1))
            for mxu in range(2):
                left_rows = jnp.concatenate(left[mxu], 0)
                pltpu.matmul_acc_lhs(accs[mxu][k % DEPTH], left_rows, 0 if k == 0 else None)

        def finish(pair, k):
            product = [pltpu.matmul_pop(accs[mxu][k % DEPTH]) for mxu in range(2)]
            for part in range(2):
                for u in range(8):
                    o = u * 16 + part * 8
                    both = jnp.concatenate([p[o : o + 8] for p in product], 0)
                    at = pl.ds(pl.multiple_of((8 * k + u) * F + pair * 16, 16), 16)
                    cross[part, at, :] = both.astype(jnp.bfloat16)

        def work(pair, first, last):
            same_rest = [same_bin & ((lane // 8) % 4 == (2 * pair + mxu) % 4) for mxu in range(2)]
            for k in range(groups):
                start(pair, k, same_rest)
                if not last and k == 1:
                    push(pair + 1)
                if k >= LAG:
                    finish(pair, k - LAG)
                elif not first:
                    finish(pair - 1, k - LAG + groups)

        push(0)
        work(0, True, False)
        pl.loop(1, NB // 2 - 1)(lambda pair: work(pair, False, False))
        work(NB // 2 - 1, False, True)
        for k in range(groups - LAG, groups):
            finish(NB // 2 - 1, k)

    def out_copy(k):
        at = pl.ds(pl.multiple_of(row_places[k] * OWN, OWN), OWN)
        return pltpu.make_async_copy(staged.at[k % 2], out_ref.at[:, at, :], sems.at[k % 2])

    def emit(g):
        if g >= 2:
            out_copy(g - 2).wait()
        for lag in range(HALF + 1):
            for h in range(2):
                e, o = (lagged[2 * (g % TOGETHER) + part][h, pl.ds(lag, OWN, stride=LAG_ROWS), :] for part in range(2))
                lanes = slice(h * 128, (h + 1) * 128)
                staged[g % 2, HALF + lag, :, lanes] = ((e + o) * (1.0 / math.sqrt(W * F))).astype(jnp.bfloat16)
                if lag:
                    staged[g % 2, HALF - lag, :, lanes] = ((e - o) * (1.0 / math.sqrt(W * F))).astype(jnp.bfloat16)
        out_copy(g).start()

    def lags_of(*accs):
        def acc_of(part, g, u):
            return accs[(part * TOGETHER + g % TOGETHER) * 4 + u % 4]

        def finish(g, u):
            for part in range(2):
                z = pltpu.matmul_pop(acc_of(part, g, u))
                for h in range(2):
                    rows_of = slice(u * LAG_ROWS, (u + 1) * LAG_ROWS)
                    lagged[2 * (g % TOGETHER) + part][h, rows_of, :] = z[:LAG_ROWS, h * 128 : (h + 1) * 128]

        for first in range(0, n_rows, TOGETHER):
            done = -1
            for t in range(OWN * F // 256):
                channels = [(k, u) for k, (tile, u) in enumerate(segments()) if tile == t]
                tables = [[table_ref[part, k] for part in range(2)] for k, _ in channels]
                for g in range(first, first + TOGETHER):
                    at = g * OWN * F + t * 256
                    staged_in = (t * TOGETHER + g) % 2
                    for part in range(2):
                        pltpu.matmul_push_rhs(cross[part, at : at + 256, :], staged_in, part)
                    for n, (k, u) in enumerate(channels):
                        for part in range(2):
                            pltpu.matmul_acc_lhs(acc_of(part, g, u), tables[n][part], None if n else staged_in)
                while done < channels[-1][1] - 2:
                    done += 1
                    for g in range(first, first + TOGETHER):
                        finish(g, done)
            for u in range(done + 1, OWN):
                for g in range(first, first + TOGETHER):
                    finish(g, u)
            for g in range(first, first + TOGETHER):
                emit(g)

    pl.run_scoped(cross_of, *[pltpu.ACC(mxu)((128, 256), jnp.float32) for mxu in [0] * DEPTH + [1] * DEPTH])
    loads[-1].wait()
    pl.run_scoped(lags_of, *[pltpu.ACC(mxu)((LAG_TILE, 256), jnp.float32) for mxu in [0] * (4 * TOGETHER) + [1] * (4 * TOGETHER)])
    for k in range(n_rows - 2, n_rows):
        out_copy(k).wait()


def correlate(rows, cols, swapped, shape, kept=()):
    row_blocks, col_blocks = list(rows.values()), list(cols.values()) + [swapped[key] for key in cols]
    n, m = OWN * len(row_blocks), OWN * len(col_blocks)
    vmem, anywhere = pl.BlockSpec(memory_space=pltpu.VMEM), pl.BlockSpec(memory_space=pl.ANY)
    inputs = (*row_blocks, *col_blocks, jnp.asarray(lag_tables(), jnp.bfloat16), *kept)
    return pl.pallas_call(
        functools.partial(correlate_kernel, tuple(rows), tuple(cols), len(kept)),
        in_specs=[vmem] * len(row_blocks) + [anywhere] * (len(col_blocks) + 1 + len(kept)),
        out_specs=anywhere,
        out_shape=jax.ShapeDtypeStruct(shape, jnp.bfloat16),
        input_output_aliases={len(inputs) - 1: 0} if kept else {},
        scratch_shapes=[
            pltpu.VMEM((m, LANES), jnp.bfloat16),
            pltpu.VMEM((2, len(segments()), LAG_TILE, 256), jnp.bfloat16),
            pltpu.VMEM((n, LANES), jnp.float32),
            pltpu.VMEM((n, LANES), jnp.float32),
            pltpu.VMEM((2, n * F, m), jnp.bfloat16),
            *[pltpu.VMEM((2, OWN * LAG_ROWS, 128), jnp.float32)] * (2 * TOGETHER),
            pltpu.VMEM((2, LAGS, OWN, m), jnp.bfloat16),
            pltpu.SemaphoreType.DMA((2,)),
            pltpu.SemaphoreType.DMA((len(col_blocks) + 1,)),
        ],
        compiler_params=pltpu.CompilerParams(vmem_limit_bytes=52 * 1024 * 1024),
        cost_estimate=pl.CostEstimate(flops=n * 2 * 10**8, bytes_accessed=10**7, transcendentals=0),
    )(*inputs)


def near(block, side, move):
    return {(0, 0): block, (0, 1): side, (-1, 0): move(block, 1, 0), (1, 0): move(block, -1, 0)}


def far(found, move):
    return {
        (-1, 1): move(found[0, 1], 1, 0),
        (1, 1): move(found[0, 1], -1, 0),
        (2, 0): move(found[-1, 0], 1, 0),
        (2, 1): move(found[1, 0], -1, 1),
    }


def body(spectra, offsets, channel_mask):
    white = whiten(spectra, offsets, channel_mask)

    def over_rcv(value, ring, side):
        return lax.ppermute(value, "rcv", [(i, step(i, ring, side)) for i in range(8)])

    def over_src(value, ring, side):
        return lax.ppermute(value, "src", [(i, 2 * step(i // 2, ring, side) + i % 2) for i in range(16)])

    def other_core(value):
        return lax.ppermute(value, "src", [(i, i ^ 1) for i in range(16)])

    flip = [
        ((i * 2 + k) * 8 + step(j, 2, 0), (j * 2 + k) * 8 + i) for i in range(8) for k in range(2) for j in range(8)
    ]
    turned = lax.ppermute(white, ("src", "rcv"), flip)
    white, side, turned = lax.optimization_barrier((white, over_rcv(white, 0, 1), turned))
    cols = near(turned, over_src(turned, 0, 1), over_src)
    rows, cols = lax.optimization_barrier((near(white, side, over_rcv), cols))
    cols |= far(cols, over_src)
    swapped = {key: other_core(value) for key, value in cols.items()}
    shape = (LAGS, 8 * OWN, 16 * OWN)
    first = correlate(rows, cols, swapped, shape)
    return correlate(far(rows, over_rcv), cols, swapped, shape, (first,))


def solution(mesh):
    in_specs = (P(("src", "rcv"), None, None, None), P(("src", "rcv"), None), P(("src", "rcv")))
    out_specs = P(None, "src", "rcv")
    return jax.shard_map(body, mesh=mesh, in_specs=in_specs, out_specs=out_specs, check_vma=False)
```

```python
import functools
import math

import jax
import jax.numpy as jnp
import numpy as np
from jax import lax
from jax.experimental import pallas as pl
from jax.experimental.pallas import tpu as pltpu
from jax.sharding import PartitionSpec as P

W = 10
F = 400
KLO = 6
NT = 12000
HALF = 50
LAGS = 2 * HALF + 1
LAG_ROWS = 56
LAG_TILE = 64
UNROLL = 10
TOGETHER = 2
FB = 8
NB = F // FB
OWN = 16
MAIN = 16
TILES = NB + -(-NB // 4)
LANES = TILES * 128
DEPTH = 8
LAG = 4


def unit_circle(turns):
    turns = turns - NT * jnp.floor(turns * (1.0 / NT))
    quarter = jnp.floor(turns * (4.0 / NT) + 0.5)
    a = (turns - (NT // 4) * quarter) * (2.0 * math.pi / NT)
    s = a * a
    sin = a + a * s * (-1 / 6 + s * (1 / 120 + s * (-1 / 5040 + s * (1 / 362880))))
    cos = 1.0 + s * (-0.5 + s * (1 / 24 + s * (-1 / 720 + s * (1 / 40320 + s * (-1 / 3628800)))))
    swap = (quarter == 1.0) | (quarter == 3.0)
    c = jnp.where(swap, sin, cos)
    s = jnp.where(swap, cos, sin)
    c = jnp.where((quarter == 1.0) | (quarter == 2.0), -c, c)
    s = jnp.where((quarter == 2.0) | (quarter == 3.0), -s, s)
    return c, s


def whiten_kernel(mask_ref, spectra_ref, offsets_ref, white_ref, parts):
    freq = (KLO + lax.broadcasted_iota(jnp.int32, (W, F), 1)).astype(jnp.float32)
    eye = lax.broadcasted_iota(jnp.int32, (W, W), 0) == lax.broadcasted_iota(jnp.int32, (W, W), 1)
    parts[3] = jnp.zeros((OWN * 32, 128), jnp.float32)
    for ch in range(OWN):
        re = spectra_ref[ch, 0].astype(jnp.float32)
        im = spectra_ref[ch, 1].astype(jnp.float32)
        power = jnp.sum(re * re + im * im, axis=1, keepdims=True) * (1.0 / F)
        scale = lax.rsqrt(power + 1e-06) * mask_ref[ch].astype(jnp.float32)
        row = jnp.broadcast_to(offsets_ref[ch : ch + 1].astype(jnp.float32), (W, W))
        offset = jnp.sum(jnp.where(eye, row, 0.0), axis=1, keepdims=True)
        c, s = unit_circle(offset * freq)
        out = ((re * c + im * s) * scale, (im * c - re * s) * scale)
        for part in range(2):
            for t in range(4):
                n = min(128, F - 128 * t)
                parts[t, ch * 32 + part * 16 : ch * 32 + part * 16 + W, :n] = out[part][:, 128 * t : 128 * t + n]

    chunk = lax.broadcasted_iota(jnp.int32, (OWN, 128), 1) // 8
    for t in range(4):
        pairs = [parts[t, pl.ds(16 * (m % 2) + m // 2, OWN, stride=32), :] for m in range(2 * W)]
        main, rest = pairs[:MAIN], pairs[MAIN:]
        for values, low, bits in ((main, 0, 4), (rest, 2, 2)):
            for bit in range(bits):
                shift = 8 << (low + bit)
                upper = (chunk >> (low + bit)) % 2 == 1
                for m in range(len(values)):
                    if not m >> bit & 1:
                        a, b = values[m], values[m | 1 << bit]
                        values[m] = jnp.where(upper, pltpu.roll(b, shift, 1), a)
                        values[m | 1 << bit] = jnp.where(upper, b, pltpu.roll(a, 128 - shift, 1))
        for k in range(16):
            if 16 * t + k < NB:
                white_ref[:, (16 * t + k) * 128 : (16 * t + k + 1) * 128] = main[k].astype(jnp.bfloat16)
        for k in range(4):
            tile = NB + 4 * t + k
            if tile < TILES:
                white_ref[:, tile * 128 : (tile + 1) * 128] = rest[k].astype(jnp.bfloat16)


def whiten(spectra, offsets, channel_mask):
    return pl.pallas_call(
        whiten_kernel,
        in_specs=[
            pl.BlockSpec(memory_space=pltpu.SMEM),
            pl.BlockSpec(memory_space=pltpu.VMEM),
            pl.BlockSpec(memory_space=pltpu.VMEM),
        ],
        out_specs=pl.BlockSpec(memory_space=pltpu.VMEM),
        out_shape=jax.ShapeDtypeStruct((OWN, LANES), jnp.bfloat16),
        scratch_shapes=[pltpu.VMEM((4, OWN * 32, 128), jnp.float32)],
    )(channel_mask, spectra, offsets)


def segments():
    return [(t, u) for t in range(OWN * F // 256) for u in range(256 * t // F, (256 * t + 255) // F + 1)]


def lag_tables():
    freq = KLO + np.arange(F)
    angle = 2.0 * math.pi / NT * ((np.arange(HALF + 1)[:, None] * freq[None, :]) % NT)
    tables = np.pad(np.stack([np.cos(angle), -np.sin(angle)]), ((0, 0), (0, LAG_TILE - HALF - 1), (256, 256)))
    return np.stack([tables[:, :, 256 + 256 * t - F * u :][:, :, :256] for t, u in segments()], 1)


def step(index, ring, side):
    return (index ^ (4 * side)) & 4 | (index + ring) & 3


def correlate_kernel(row_keys, col_keys, n_kept, *refs):
    n_rows, n_cols = len(row_keys), 2 * len(col_keys)
    p, q, core = lax.axis_index("rcv"), lax.axis_index("src") // 2, lax.axis_index("src") % 2
    row_places = [step(p, *key) for key in row_keys]
    col_places = [c * 8 + step(step(q, *key), 2, 0) for c in (core, 1 - core) for key in col_keys]
    row_refs, refs = refs[:n_rows], refs[n_rows:]
    col_refs, refs = refs[:n_cols], refs[n_cols:]
    table_from, out_ref, cols, table_ref, rows, turned, cross, *lagged, staged, sems, in_sems = (
        refs[:1] + refs[1 + n_kept :]
    )
    lane = lax.broadcasted_iota(jnp.int32, (16, 128), 1)
    same_bin = (lane % 8) == lax.broadcasted_iota(jnp.int32, (16, 128), 0) % 8
    zero = jnp.zeros((), jnp.bfloat16)
    groups = n_rows * OWN // 8

    loads = []
    for k, ref in enumerate(col_refs):
        at = pl.ds(pl.multiple_of(col_places[k] * OWN, OWN), OWN)
        loads.append(pltpu.make_async_copy(ref, cols.at[at, :], in_sems.at[k]))
    loads.append(pltpu.make_async_copy(table_from, table_ref, in_sems.at[n_cols]))
    for load in loads:
        load.start()

    def spread(first, last, shift):
        minus = (lax.broadcasted_iota(jnp.int32, (OWN, 128), 1) // shift) % 2 == 1

        @pl.loop(first, last, unroll=UNROLL)
        def _(t):
            at = pl.ds(pl.multiple_of(t * 128, 128), 128)
            for k, ref in enumerate(row_refs):
                v = ref[:, at].astype(jnp.float32)
                rows[k * OWN : (k + 1) * OWN, at] = v
                v = jnp.where(minus, -pltpu.roll(v, shift, 1), pltpu.roll(v, 128 - shift, 1))
                turned[k * OWN : (k + 1) * OWN, at] = v

    spread(0, NB, 8)
    spread(NB, TILES, 32)
    for load in loads[:-1]:
        load.wait()

    def cross_of(*accs):
        accs = accs[:DEPTH], accs[DEPTH:]

        def main_lanes(b):
            return pl.ds(pl.multiple_of(b * 128, 128), 128)

        def rest_lanes(pair):
            return pl.ds(pl.multiple_of((NB + pair // 2) * 128, 128), 128)

        def push(pair):
            for mxu in range(2):
                right = jnp.concatenate([cols[:, main_lanes(2 * pair + mxu)], cols[:, rest_lanes(pair)]], 1)
                pltpu.matmul_push_rhs(right, 0, mxu, transpose=True)

        def wide(i, lanes):
            both = [jnp.broadcast_to(ref[i : i + 1, lanes], (8, 128)) for ref in (rows, turned)]
            return jnp.concatenate(both, 0).astype(jnp.bfloat16)

        def start(pair, k, same_rest):
            left = [], []
            for u in range(8):
                r = wide(8 * k + u, rest_lanes(pair))
                for mxu in range(2):
                    m = wide(8 * k + u, main_lanes(2 * pair + mxu))
                    m, q = jnp.where(same_bin, m, zero), jnp.where(same_rest[mxu], r, zero)
                    left[mxu].append(jnp.concatenate([m, q], 1))
            for mxu in range(2):
                left_rows = jnp.concatenate(left[mxu], 0)
                pltpu.matmul_acc_lhs(accs[mxu][k % DEPTH], left_rows, 0 if k == 0 else None)

        def finish(pair, k):
            product = [pltpu.matmul_pop(accs[mxu][k % DEPTH]) for mxu in range(2)]
            for part in range(2):
                for u in range(8):
                    o = u * 16 + part * 8
                    both = jnp.concatenate([p[o : o + 8] for p in product], 0)
                    at = pl.ds(pl.multiple_of((8 * k + u) * F + pair * 16, 16), 16)
                    cross[part, at, :] = both.astype(jnp.bfloat16)

        def work(pair, first, last):
            same_rest = [same_bin & ((lane // 8) % 4 == (2 * pair + mxu) % 4) for mxu in range(2)]
            for k in range(groups):
                start(pair, k, same_rest)
                if not last and k == 1:
                    push(pair + 1)
                if k >= LAG:
                    finish(pair, k - LAG)
                elif not first:
                    finish(pair - 1, k - LAG + groups)

        push(0)
        work(0, True, False)
        pl.loop(1, NB // 2 - 1)(lambda pair: work(pair, False, False))
        work(NB // 2 - 1, False, True)
        for k in range(groups - LAG, groups):
            finish(NB // 2 - 1, k)

    def out_copy(k):
        at = pl.ds(pl.multiple_of(row_places[k] * OWN, OWN), OWN)
        return pltpu.make_async_copy(staged.at[k % 2], out_ref.at[:, at, :], sems.at[k % 2])

    def emit(g):
        if g >= 2:
            out_copy(g - 2).wait()
        for lag in range(HALF + 1):
            for h in range(2):
                e, o = (lagged[2 * (g % TOGETHER) + part][h, pl.ds(lag, OWN, stride=LAG_ROWS), :] for part in range(2))
                lanes = slice(h * 128, (h + 1) * 128)
                staged[g % 2, HALF + lag, :, lanes] = ((e + o) * (1.0 / math.sqrt(W * F))).astype(jnp.bfloat16)
                if lag:
                    staged[g % 2, HALF - lag, :, lanes] = ((e - o) * (1.0 / math.sqrt(W * F))).astype(jnp.bfloat16)
        out_copy(g).start()

    def lags_of(*accs):
        def acc_of(part, g, u):
            return accs[(part * TOGETHER + g % TOGETHER) * 4 + u % 4]

        def finish(g, u):
            for part in range(2):
                z = pltpu.matmul_pop(acc_of(part, g, u))
                for h in range(2):
                    rows_of = slice(u * LAG_ROWS, (u + 1) * LAG_ROWS)
                    lagged[2 * (g % TOGETHER) + part][h, rows_of, :] = z[:LAG_ROWS, h * 128 : (h + 1) * 128]

        for first in range(0, n_rows, TOGETHER):
            done = -1
            for t in range(OWN * F // 256):
                channels = [(k, u) for k, (tile, u) in enumerate(segments()) if tile == t]
                tables = [[table_ref[part, k] for part in range(2)] for k, _ in channels]
                for g in range(first, first + TOGETHER):
                    at = g * OWN * F + t * 256
                    staged_in = (t * TOGETHER + g) % 2
                    for part in range(2):
                        pltpu.matmul_push_rhs(cross[part, at : at + 256, :], staged_in, part)
                    for n, (k, u) in enumerate(channels):
                        for part in range(2):
                            pltpu.matmul_acc_lhs(acc_of(part, g, u), tables[n][part], None if n else staged_in)
                while done < channels[-1][1] - 2:
                    done += 1
                    for g in range(first, first + TOGETHER):
                        finish(g, done)
            for u in range(done + 1, OWN):
                for g in range(first, first + TOGETHER):
                    finish(g, u)
            for g in range(first, first + TOGETHER):
                emit(g)

    pl.run_scoped(cross_of, *[pltpu.ACC(mxu)((128, 256), jnp.float32) for mxu in [0] * DEPTH + [1] * DEPTH])
    loads[-1].wait()
    pl.run_scoped(lags_of, *[pltpu.ACC(mxu)((LAG_TILE, 256), jnp.float32) for mxu in [0] * (4 * TOGETHER) + [1] * (4 * TOGETHER)])
    for k in range(n_rows - 2, n_rows):
        out_copy(k).wait()


def correlate(rows, cols, swapped, shape, kept=()):
    row_blocks, col_blocks = list(rows.values()), list(cols.values()) + [swapped[key] for key in cols]
    n, m = OWN * len(row_blocks), OWN * len(col_blocks)
    vmem, anywhere = pl.BlockSpec(memory_space=pltpu.VMEM), pl.BlockSpec(memory_space=pl.ANY)
    inputs = (*row_blocks, *col_blocks, jnp.asarray(lag_tables(), jnp.bfloat16), *kept)
    return pl.pallas_call(
        functools.partial(correlate_kernel, tuple(rows), tuple(cols), len(kept)),
        in_specs=[vmem] * len(row_blocks) + [anywhere] * (len(col_blocks) + 1 + len(kept)),
        out_specs=anywhere,
        out_shape=jax.ShapeDtypeStruct(shape, jnp.bfloat16),
        input_output_aliases={len(inputs) - 1: 0} if kept else {},
        scratch_shapes=[
            pltpu.VMEM((m, LANES), jnp.bfloat16),
            pltpu.VMEM((2, len(segments()), LAG_TILE, 256), jnp.bfloat16),
            pltpu.VMEM((n, LANES), jnp.float32),
            pltpu.VMEM((n, LANES), jnp.float32),
            pltpu.VMEM((2, n * F, m), jnp.bfloat16),
            *[pltpu.VMEM((2, OWN * LAG_ROWS, 128), jnp.float32)] * (2 * TOGETHER),
            pltpu.VMEM((2, LAGS, OWN, m), jnp.bfloat16),
            pltpu.SemaphoreType.DMA((2,)),
            pltpu.SemaphoreType.DMA((len(col_blocks) + 1,)),
        ],
        compiler_params=pltpu.CompilerParams(vmem_limit_bytes=45 * 1024 * 1024),
        cost_estimate=pl.CostEstimate(flops=n * 2 * 10**8, bytes_accessed=10**7, transcendentals=0),
    )(*inputs)


def near(block, side, move):
    return {(0, 0): block, (0, 1): side, (-1, 0): move(block, 1, 0), (1, 0): move(block, -1, 0)}


def far(found, move):
    return {
        (-1, 1): move(found[0, 1], 1, 0),
        (1, 1): move(found[0, 1], -1, 0),
        (2, 0): move(found[-1, 0], 1, 0),
        (2, 1): move(found[1, 0], -1, 1),
    }


def body(spectra, offsets, channel_mask):
    white = whiten(spectra, offsets, channel_mask)

    def over_rcv(value, ring, side):
        return lax.ppermute(value, "rcv", [(i, step(i, ring, side)) for i in range(8)])

    def over_src(value, ring, side):
        return lax.ppermute(value, "src", [(i, 2 * step(i // 2, ring, side) + i % 2) for i in range(16)])

    def other_core(value):
        return lax.ppermute(value, "src", [(i, i ^ 1) for i in range(16)])

    flip = [
        ((i * 2 + k) * 8 + step(j, 2, 0), (j * 2 + k) * 8 + i) for i in range(8) for k in range(2) for j in range(8)
    ]
    turned = lax.ppermute(white, ("src", "rcv"), flip)
    white, side, turned = lax.optimization_barrier((white, over_rcv(white, 0, 1), turned))
    cols = near(turned, over_src(turned, 0, 1), over_src)
    rows, cols = lax.optimization_barrier((near(white, side, over_rcv), cols))
    cols |= far(cols, over_src)
    swapped = {key: other_core(value) for key, value in cols.items()}
    shape = (LAGS, 8 * OWN, 16 * OWN)
    first = correlate(rows, cols, swapped, shape)
    return correlate(far(rows, over_rcv), cols, swapped, shape, (first,))


def solution(mesh):
    in_specs = (P(("src", "rcv"), None, None, None), P(("src", "rcv"), None), P(("src", "rcv")))
    out_specs = P(None, "src", "rcv")
    return jax.shard_map(body, mesh=mesh, in_specs=in_specs, out_specs=out_specs, check_vma=False)
```

```python
import functools
import math

import jax
import jax.numpy as jnp
import numpy as np
from jax import lax
from jax.experimental import pallas as pl
from jax.experimental.pallas import tpu as pltpu
from jax.sharding import PartitionSpec as P

W = 10
F = 400
KLO = 6
NT = 12000
HALF = 50
LAGS = 2 * HALF + 1
LAG_ROWS = 56
LAG_TILE = 64
UNROLL = 10
TOGETHER = 2
FB = 8
NB = F // FB
OWN = 16
MAIN = 16
TILES = NB + -(-NB // 4)
LANES = TILES * 128
SOME = 4
DEPTH = 8
LAG = 6


def unit_circle(turns):
    turns = turns - NT * jnp.floor(turns * (1.0 / NT))
    quarter = jnp.floor(turns * (4.0 / NT) + 0.5)
    a = (turns - (NT // 4) * quarter) * (2.0 * math.pi / NT)
    s = a * a
    sin = a + a * s * (-1 / 6 + s * (1 / 120 + s * (-1 / 5040 + s * (1 / 362880))))
    cos = 1.0 + s * (-0.5 + s * (1 / 24 + s * (-1 / 720 + s * (1 / 40320 + s * (-1 / 3628800)))))
    swap = (quarter == 1.0) | (quarter == 3.0)
    c = jnp.where(swap, sin, cos)
    s = jnp.where(swap, cos, sin)
    c = jnp.where((quarter == 1.0) | (quarter == 2.0), -c, c)
    s = jnp.where((quarter == 2.0) | (quarter == 3.0), -s, s)
    return c, s


def whiten_kernel(mask_ref, spectra_ref, offsets_ref, white_ref, parts):
    freq = (KLO + lax.broadcasted_iota(jnp.int32, (W, F), 1)).astype(jnp.float32)
    eye = lax.broadcasted_iota(jnp.int32, (W, W), 0) == lax.broadcasted_iota(jnp.int32, (W, W), 1)
    parts[3] = jnp.zeros((OWN * 32, 128), jnp.float32)
    for ch in range(OWN):
        re = spectra_ref[ch, 0].astype(jnp.float32)
        im = spectra_ref[ch, 1].astype(jnp.float32)
        power = jnp.sum(re * re + im * im, axis=1, keepdims=True) * (1.0 / F)
        scale = lax.rsqrt(power + 1e-06) * mask_ref[ch].astype(jnp.float32)
        row = jnp.broadcast_to(offsets_ref[ch : ch + 1].astype(jnp.float32), (W, W))
        offset = jnp.sum(jnp.where(eye, row, 0.0), axis=1, keepdims=True)
        c, s = unit_circle(offset * freq)
        out = ((re * c + im * s) * scale, (im * c - re * s) * scale)
        for part in range(2):
            for t in range(4):
                n = min(128, F - 128 * t)
                parts[t, ch * 32 + part * 16 : ch * 32 + part * 16 + W, :n] = out[part][:, 128 * t : 128 * t + n]

    chunk = lax.broadcasted_iota(jnp.int32, (OWN, 128), 1) // 8
    for t in range(4):
        pairs = [parts[t, pl.ds(16 * (m % 2) + m // 2, OWN, stride=32), :] for m in range(2 * W)]
        main, rest = pairs[:MAIN], pairs[MAIN:]
        for values, low, bits in ((main, 0, 4), (rest, 2, 2)):
            for bit in range(bits):
                shift = 8 << (low + bit)
                upper = (chunk >> (low + bit)) % 2 == 1
                for m in range(len(values)):
                    if not m >> bit & 1:
                        a, b = values[m], values[m | 1 << bit]
                        values[m] = jnp.where(upper, pltpu.roll(b, shift, 1), a)
                        values[m | 1 << bit] = jnp.where(upper, b, pltpu.roll(a, 128 - shift, 1))
        for k in range(16):
            if 16 * t + k < NB:
                white_ref[:, (16 * t + k) * 128 : (16 * t + k + 1) * 128] = main[k].astype(jnp.bfloat16)
        for k in range(4):
            tile = NB + 4 * t + k
            if tile < TILES:
                white_ref[:, tile * 128 : (tile + 1) * 128] = rest[k].astype(jnp.bfloat16)


def whiten(spectra, offsets, channel_mask):
    return pl.pallas_call(
        whiten_kernel,
        in_specs=[
            pl.BlockSpec(memory_space=pltpu.SMEM),
            pl.BlockSpec(memory_space=pltpu.VMEM),
            pl.BlockSpec(memory_space=pltpu.VMEM),
        ],
        out_specs=pl.BlockSpec(memory_space=pltpu.VMEM),
        out_shape=jax.ShapeDtypeStruct((OWN, LANES), jnp.bfloat16),
        scratch_shapes=[pltpu.VMEM((4, OWN * 32, 128), jnp.float32)],
    )(channel_mask, spectra, offsets)


def segments():
    return [(t, u) for t in range(OWN * F // 256) for u in range(256 * t // F, (256 * t + 255) // F + 1)]


def lag_tables():
    freq = KLO + np.arange(F)
    angle = 2.0 * math.pi / NT * ((np.arange(HALF + 1)[:, None] * freq[None, :]) % NT)
    tables = np.pad(np.stack([np.cos(angle), -np.sin(angle)]), ((0, 0), (0, LAG_TILE - HALF - 1), (256, 256)))
    return np.stack([tables[:, :, 256 + 256 * t - F * u :][:, :, :256] for t, u in segments()], 1)


def step(index, ring, side):
    return (index ^ (4 * side)) & 4 | (index + ring) & 3


def correlate_kernel(row_keys, col_keys, n_kept, *refs):
    n_rows, n_cols = len(row_keys), 2 * len(col_keys)
    p, q, core = lax.axis_index("rcv"), lax.axis_index("src") // 2, lax.axis_index("src") % 2
    row_places = [step(p, *key) for key in row_keys]
    col_places = [c * 8 + step(step(q, *key), 2, 0) for c in (core, 1 - core) for key in col_keys]
    row_refs, refs = refs[:n_rows], refs[n_rows:]
    col_refs, refs = refs[:n_cols], refs[n_cols:]
    table_from, out_ref, cols, table_ref, rows, turned, cross, *lagged, staged, sems, in_sems = (
        refs[:1] + refs[1 + n_kept :]
    )
    lane = lax.broadcasted_iota(jnp.int32, (16, 128), 1)
    same_bin = (lane % 8) == lax.broadcasted_iota(jnp.int32, (16, 128), 0) % 8
    zero = jnp.zeros((), jnp.bfloat16)
    groups = n_rows * OWN // SOME

    loads = []
    for k, ref in enumerate(col_refs):
        at = pl.ds(pl.multiple_of(col_places[k] * OWN, OWN), OWN)
        loads.append(pltpu.make_async_copy(ref, cols.at[at, :], in_sems.at[k]))
    loads.append(pltpu.make_async_copy(table_from, table_ref, in_sems.at[n_cols]))
    for load in loads:
        load.start()

    def spread(first, last, shift):
        minus = (lax.broadcasted_iota(jnp.int32, (OWN, 128), 1) // shift) % 2 == 1

        @pl.loop(first, last, unroll=UNROLL)
        def _(t):
            at = pl.ds(pl.multiple_of(t * 128, 128), 128)
            for k, ref in enumerate(row_refs):
                v = ref[:, at].astype(jnp.float32)
                rows[k * OWN : (k + 1) * OWN, at] = v
                v = jnp.where(minus, -pltpu.roll(v, shift, 1), pltpu.roll(v, 128 - shift, 1))
                turned[k * OWN : (k + 1) * OWN, at] = v

    spread(0, NB, 8)
    spread(NB, TILES, 32)
    for load in loads[:-1]:
        load.wait()

    def cross_of(*accs):
        accs = accs[:DEPTH], accs[DEPTH:]

        def main_lanes(b):
            return pl.ds(pl.multiple_of(b * 128, 128), 128)

        def rest_lanes(pair):
            return pl.ds(pl.multiple_of((NB + pair // 2) * 128, 128), 128)

        def push(pair):
            for mxu in range(2):
                right = jnp.concatenate([cols[:, main_lanes(2 * pair + mxu)], cols[:, rest_lanes(pair)]], 1)
                pltpu.matmul_push_rhs(right, 0, mxu, transpose=True)

        def wide(i, lanes):
            both = [jnp.broadcast_to(ref[i : i + 1, lanes], (8, 128)) for ref in (rows, turned)]
            return jnp.concatenate(both, 0).astype(jnp.bfloat16)

        def start(pair, k, same_rest):
            left = [], []
            for u in range(SOME):
                r = wide(SOME * k + u, rest_lanes(pair))
                for mxu in range(2):
                    m = wide(SOME * k + u, main_lanes(2 * pair + mxu))
                    m, q = jnp.where(same_bin, m, zero), jnp.where(same_rest[mxu], r, zero)
                    left[mxu].append(jnp.concatenate([m, q], 1))
            for mxu in range(2):
                left_rows = jnp.concatenate(left[mxu], 0)
                pltpu.matmul_acc_lhs(accs[mxu][k % DEPTH], left_rows, 0 if k == 0 else None)

        def finish(pair, k):
            product = [pltpu.matmul_pop(accs[mxu][k % DEPTH]) for mxu in range(2)]
            for part in range(2):
                for u in range(SOME):
                    o = u * 16 + part * 8
                    both = jnp.concatenate([p[o : o + 8] for p in product], 0)
                    at = pl.ds(pl.multiple_of((SOME * k + u) * F + pair * 16, 16), 16)
                    cross[part, at, :] = both.astype(jnp.bfloat16)

        def work(pair, first, last):
            same_rest = [same_bin & ((lane // 8) % 4 == (2 * pair + mxu) % 4) for mxu in range(2)]
            for k in range(groups):
                start(pair, k, same_rest)
                if not last and k == 1:
                    push(pair + 1)
                if k >= LAG:
                    finish(pair, k - LAG)
                elif not first:
                    finish(pair - 1, k - LAG + groups)

        push(0)
        work(0, True, False)
        pl.loop(1, NB // 2 - 1)(lambda pair: work(pair, False, False))
        work(NB // 2 - 1, False, True)
        for k in range(groups - LAG, groups):
            finish(NB // 2 - 1, k)

    def out_copy(k):
        at = pl.ds(pl.multiple_of(row_places[k] * OWN, OWN), OWN)
        return pltpu.make_async_copy(staged.at[k % 2], out_ref.at[:, at, :], sems.at[k % 2])

    def emit(g):
        if g >= 2:
            out_copy(g - 2).wait()
        for lag in range(HALF + 1):
            for h in range(2):
                e, o = (lagged[2 * (g % TOGETHER) + part][h, pl.ds(lag, OWN, stride=LAG_ROWS), :] for part in range(2))
                lanes = slice(h * 128, (h + 1) * 128)
                staged[g % 2, HALF + lag, :, lanes] = ((e + o) * (1.0 / math.sqrt(W * F))).astype(jnp.bfloat16)
                if lag:
                    staged[g % 2, HALF - lag, :, lanes] = ((e - o) * (1.0 / math.sqrt(W * F))).astype(jnp.bfloat16)
        out_copy(g).start()

    def lags_of(*accs):
        def acc_of(part, g, u):
            return accs[(part * TOGETHER + g % TOGETHER) * 4 + u % 4]

        def finish(g, u):
            for part in range(2):
                z = pltpu.matmul_pop(acc_of(part, g, u))
                for h in range(2):
                    rows_of = slice(u * LAG_ROWS, (u + 1) * LAG_ROWS)
                    lagged[2 * (g % TOGETHER) + part][h, rows_of, :] = z[:LAG_ROWS, h * 128 : (h + 1) * 128]

        for first in range(0, n_rows, TOGETHER):
            done = -1
            for t in range(OWN * F // 256):
                channels = [(k, u) for k, (tile, u) in enumerate(segments()) if tile == t]
                tables = [[table_ref[part, k] for part in range(2)] for k, _ in channels]
                for g in range(first, first + TOGETHER):
                    at = g * OWN * F + t * 256
                    staged_in = (t * TOGETHER + g) % 2
                    for part in range(2):
                        pltpu.matmul_push_rhs(cross[part, at : at + 256, :], staged_in, part)
                    for n, (k, u) in enumerate(channels):
                        for part in range(2):
                            pltpu.matmul_acc_lhs(acc_of(part, g, u), tables[n][part], None if n else staged_in)
                while done < channels[-1][1] - 2:
                    done += 1
                    for g in range(first, first + TOGETHER):
                        finish(g, done)
            for u in range(done + 1, OWN):
                for g in range(first, first + TOGETHER):
                    finish(g, u)
            for g in range(first, first + TOGETHER):
                emit(g)

    pl.run_scoped(cross_of, *[pltpu.ACC(mxu)((SOME * 16, 256), jnp.float32) for mxu in [0] * DEPTH + [1] * DEPTH])
    loads[-1].wait()
    pl.run_scoped(lags_of, *[pltpu.ACC(mxu)((LAG_TILE, 256), jnp.float32) for mxu in [0] * (4 * TOGETHER) + [1] * (4 * TOGETHER)])
    for k in range(n_rows - 2, n_rows):
        out_copy(k).wait()


def correlate(rows, cols, swapped, shape, kept=()):
    row_blocks, col_blocks = list(rows.values()), list(cols.values()) + [swapped[key] for key in cols]
    n, m = OWN * len(row_blocks), OWN * len(col_blocks)
    vmem, anywhere = pl.BlockSpec(memory_space=pltpu.VMEM), pl.BlockSpec(memory_space=pl.ANY)
    inputs = (*row_blocks, *col_blocks, jnp.asarray(lag_tables(), jnp.bfloat16), *kept)
    return pl.pallas_call(
        functools.partial(correlate_kernel, tuple(rows), tuple(cols), len(kept)),
        in_specs=[vmem] * len(row_blocks) + [anywhere] * (len(col_blocks) + 1 + len(kept)),
        out_specs=anywhere,
        out_shape=jax.ShapeDtypeStruct(shape, jnp.bfloat16),
        input_output_aliases={len(inputs) - 1: 0} if kept else {},
        scratch_shapes=[
            pltpu.VMEM((m, LANES), jnp.bfloat16),
            pltpu.VMEM((2, len(segments()), LAG_TILE, 256), jnp.bfloat16),
            pltpu.VMEM((n, LANES), jnp.float32),
            pltpu.VMEM((n, LANES), jnp.float32),
            pltpu.VMEM((2, n * F, m), jnp.bfloat16),
            *[pltpu.VMEM((2, OWN * LAG_ROWS, 128), jnp.float32)] * (2 * TOGETHER),
            pltpu.VMEM((2, LAGS, OWN, m), jnp.bfloat16),
            pltpu.SemaphoreType.DMA((2,)),
            pltpu.SemaphoreType.DMA((len(col_blocks) + 1,)),
        ],
        compiler_params=pltpu.CompilerParams(vmem_limit_bytes=52 * 1024 * 1024),
        cost_estimate=pl.CostEstimate(flops=n * 2 * 10**8, bytes_accessed=10**7, transcendentals=0),
    )(*inputs)


def near(block, side, move):
    return {(0, 0): block, (0, 1): side, (-1, 0): move(block, 1, 0), (1, 0): move(block, -1, 0)}


def far(found, move):
    return {
        (-1, 1): move(found[0, 1], 1, 0),
        (1, 1): move(found[0, 1], -1, 0),
        (2, 0): move(found[-1, 0], 1, 0),
        (2, 1): move(found[1, 0], -1, 1),
    }


def body(spectra, offsets, channel_mask):
    white = whiten(spectra, offsets, channel_mask)

    def over_rcv(value, ring, side):
        return lax.ppermute(value, "rcv", [(i, step(i, ring, side)) for i in range(8)])

    def over_src(value, ring, side):
        return lax.ppermute(value, "src", [(i, 2 * step(i // 2, ring, side) + i % 2) for i in range(16)])

    def other_core(value):
        return lax.ppermute(value, "src", [(i, i ^ 1) for i in range(16)])

    flip = [
        ((i * 2 + k) * 8 + step(j, 2, 0), (j * 2 + k) * 8 + i) for i in range(8) for k in range(2) for j in range(8)
    ]
    turned = lax.ppermute(white, ("src", "rcv"), flip)
    white, side, turned = lax.optimization_barrier((white, over_rcv(white, 0, 1), turned))
    cols = near(turned, over_src(turned, 0, 1), over_src)
    rows, cols = lax.optimization_barrier((near(white, side, over_rcv), cols))
    cols |= far(cols, over_src)
    swapped = {key: other_core(value) for key, value in cols.items()}
    shape = (LAGS, 8 * OWN, 16 * OWN)
    first = correlate(rows, cols, swapped, shape)
    return correlate(far(rows, over_rcv), cols, swapped, shape, (first,))


def solution(mesh):
    in_specs = (P(("src", "rcv"), None, None, None), P(("src", "rcv"), None), P(("src", "rcv")))
    out_specs = P(None, "src", "rcv")
    return jax.shard_map(body, mesh=mesh, in_specs=in_specs, out_specs=out_specs, check_vma=False)
```

```python
import functools
import math

import jax
import jax.numpy as jnp
import numpy as np
from jax import lax
from jax.experimental import pallas as pl
from jax.experimental.pallas import tpu as pltpu
from jax.sharding import PartitionSpec as P

W = 10
F = 400
KLO = 6
NT = 12000
HALF = 50
LAGS = 2 * HALF + 1
LAG_ROWS = 56
LAG_TILE = 64
UNROLL = 10
TOGETHER = 2
FB = 8
NB = F // FB
OWN = 16
MAIN = 16
TILES = NB + -(-NB // 4)
LANES = TILES * 128
SOME = 4
DEPTH = 8
LAG = 6


def unit_circle(turns):
    turns = turns - NT * jnp.floor(turns * (1.0 / NT))
    quarter = jnp.floor(turns * (4.0 / NT) + 0.5)
    a = (turns - (NT // 4) * quarter) * (2.0 * math.pi / NT)
    s = a * a
    sin = a + a * s * (-1 / 6 + s * (1 / 120 + s * (-1 / 5040 + s * (1 / 362880))))
    cos = 1.0 + s * (-0.5 + s * (1 / 24 + s * (-1 / 720 + s * (1 / 40320 + s * (-1 / 3628800)))))
    swap = (quarter == 1.0) | (quarter == 3.0)
    c = jnp.where(swap, sin, cos)
    s = jnp.where(swap, cos, sin)
    c = jnp.where((quarter == 1.0) | (quarter == 2.0), -c, c)
    s = jnp.where((quarter == 2.0) | (quarter == 3.0), -s, s)
    return c, s


def whiten_kernel(mask_ref, spectra_ref, offsets_ref, white_ref, parts):
    freq = (KLO + lax.broadcasted_iota(jnp.int32, (W, F), 1)).astype(jnp.float32)
    eye = lax.broadcasted_iota(jnp.int32, (W, W), 0) == lax.broadcasted_iota(jnp.int32, (W, W), 1)
    parts[3] = jnp.zeros((OWN * 32, 128), jnp.float32)
    for ch in range(OWN):
        re = spectra_ref[ch, 0].astype(jnp.float32)
        im = spectra_ref[ch, 1].astype(jnp.float32)
        power = jnp.sum(re * re + im * im, axis=1, keepdims=True) * (1.0 / F)
        scale = lax.rsqrt(power + 1e-06) * mask_ref[ch].astype(jnp.float32)
        row = jnp.broadcast_to(offsets_ref[ch : ch + 1].astype(jnp.float32), (W, W))
        offset = jnp.sum(jnp.where(eye, row, 0.0), axis=1, keepdims=True)
        c, s = unit_circle(offset * freq)
        out = ((re * c + im * s) * scale, (im * c - re * s) * scale)
        for part in range(2):
            for t in range(4):
                n = min(128, F - 128 * t)
                parts[t, ch * 32 + part * 16 : ch * 32 + part * 16 + W, :n] = out[part][:, 128 * t : 128 * t + n]

    chunk = lax.broadcasted_iota(jnp.int32, (OWN, 128), 1) // 8
    for t in range(4):
        pairs = [parts[t, pl.ds(16 * (m % 2) + m // 2, OWN, stride=32), :] for m in range(2 * W)]
        main, rest = pairs[:MAIN], pairs[MAIN:]
        for values, low, bits in ((main, 0, 4), (rest, 2, 2)):
            for bit in range(bits):
                shift = 8 << (low + bit)
                upper = (chunk >> (low + bit)) % 2 == 1
                for m in range(len(values)):
                    if not m >> bit & 1:
                        a, b = values[m], values[m | 1 << bit]
                        values[m] = jnp.where(upper, pltpu.roll(b, shift, 1), a)
                        values[m | 1 << bit] = jnp.where(upper, b, pltpu.roll(a, 128 - shift, 1))
        for k in range(16):
            if 16 * t + k < NB:
                white_ref[:, (16 * t + k) * 128 : (16 * t + k + 1) * 128] = main[k].astype(jnp.bfloat16)
        for k in range(4):
            tile = NB + 4 * t + k
            if tile < TILES:
                white_ref[:, tile * 128 : (tile + 1) * 128] = rest[k].astype(jnp.bfloat16)


def whiten(spectra, offsets, channel_mask):
    return pl.pallas_call(
        whiten_kernel,
        in_specs=[
            pl.BlockSpec(memory_space=pltpu.SMEM),
            pl.BlockSpec(memory_space=pltpu.VMEM),
            pl.BlockSpec(memory_space=pltpu.VMEM),
        ],
        out_specs=pl.BlockSpec(memory_space=pltpu.VMEM),
        out_shape=jax.ShapeDtypeStruct((OWN, LANES), jnp.bfloat16),
        scratch_shapes=[pltpu.VMEM((4, OWN * 32, 128), jnp.float32)],
    )(channel_mask, spectra, offsets)


def segments():
    return [(t, u) for t in range(OWN * F // 256) for u in range(256 * t // F, (256 * t + 255) // F + 1)]


def lag_tables():
    freq = KLO + np.arange(F)
    angle = 2.0 * math.pi / NT * ((np.arange(HALF + 1)[:, None] * freq[None, :]) % NT)
    tables = np.pad(np.stack([np.cos(angle), -np.sin(angle)]), ((0, 0), (0, LAG_TILE - HALF - 1), (256, 256)))
    return np.stack([tables[:, :, 256 + 256 * t - F * u :][:, :, :256] for t, u in segments()], 1)


def step(index, ring, side):
    return (index ^ (4 * side)) & 4 | (index + ring) & 3


def correlate_kernel(row_keys, col_keys, n_kept, *refs):
    n_rows, n_cols = len(row_keys), 2 * len(col_keys)
    p, q, core = lax.axis_index("rcv"), lax.axis_index("src") // 2, lax.axis_index("src") % 2
    row_places = [step(p, *key) for key in row_keys]
    col_places = [c * 8 + step(step(q, *key), 2, 0) for c in (core, 1 - core) for key in col_keys]
    row_refs, refs = refs[:n_rows], refs[n_rows:]
    col_refs, refs = refs[:n_cols], refs[n_cols:]
    table_from, out_ref, cols, table_ref, rows, turned, cross, *lagged, staged, sems, in_sems = (
        refs[:1] + refs[1 + n_kept :]
    )
    lane = lax.broadcasted_iota(jnp.int32, (16, 128), 1)
    same_bin = (lane % 8) == lax.broadcasted_iota(jnp.int32, (16, 128), 0) % 8
    zero = jnp.zeros((), jnp.bfloat16)
    groups = n_rows * OWN // SOME

    loads = []
    for k, ref in enumerate(col_refs):
        at = pl.ds(pl.multiple_of(col_places[k] * OWN, OWN), OWN)
        loads.append(pltpu.make_async_copy(ref, cols.at[at, :], in_sems.at[k]))
    loads.append(pltpu.make_async_copy(table_from, table_ref, in_sems.at[n_cols]))
    for load in loads:
        load.start()

    def spread(first, last, shift):
        minus = (lax.broadcasted_iota(jnp.int32, (OWN, 128), 1) // shift) % 2 == 1

        @pl.loop(first, last, unroll=UNROLL)
        def _(t):
            at = pl.ds(pl.multiple_of(t * 128, 128), 128)
            for k, ref in enumerate(row_refs):
                v = ref[:, at].astype(jnp.float32)
                rows[k * OWN : (k + 1) * OWN, at] = v
                v = jnp.where(minus, -pltpu.roll(v, shift, 1), pltpu.roll(v, 128 - shift, 1))
                turned[k * OWN : (k + 1) * OWN, at] = v

    spread(0, NB, 8)
    spread(NB, TILES, 32)
    for load in loads[:-1]:
        load.wait()

    def cross_of(*accs):
        accs = accs[:DEPTH], accs[DEPTH:]

        def main_lanes(b):
            return pl.ds(pl.multiple_of(b * 128, 128), 128)

        def rest_lanes(pair):
            return pl.ds(pl.multiple_of((NB + pair // 2) * 128, 128), 128)

        def push(pair):
            for mxu in range(2):
                right = jnp.concatenate([cols[:, main_lanes(2 * pair + mxu)], cols[:, rest_lanes(pair)]], 1)
                pltpu.matmul_push_rhs(right, 0, mxu, transpose=True)

        def wide(i, lanes):
            both = [jnp.broadcast_to(ref[i : i + 1, lanes], (8, 128)) for ref in (rows, turned)]
            return jnp.concatenate(both, 0).astype(jnp.bfloat16)

        def start(pair, k, same_rest):
            left = [], []
            for u in range(SOME):
                r = wide(SOME * k + u, rest_lanes(pair))
                for mxu in range(2):
                    m = wide(SOME * k + u, main_lanes(2 * pair + mxu))
                    m, q = jnp.where(same_bin, m, zero), jnp.where(same_rest[mxu], r, zero)
                    left[mxu].append(jnp.concatenate([m, q], 1))
            for mxu in range(2):
                left_rows = jnp.concatenate(left[mxu], 0)
                pltpu.matmul_acc_lhs(accs[mxu][k % DEPTH], left_rows, 0 if k == 0 else None)

        def finish(pair, k):
            product = [pltpu.matmul_pop(accs[mxu][k % DEPTH]) for mxu in range(2)]
            for part in range(2):
                for u in range(SOME):
                    o = u * 16 + part * 8
                    both = jnp.concatenate([p[o : o + 8] for p in product], 0)
                    at = pl.ds(pl.multiple_of((SOME * k + u) * F + pair * 16, 16), 16)
                    cross[part, at, :] = both.astype(jnp.bfloat16)

        def work(pair, first, last):
            same_rest = [same_bin & ((lane // 8) % 4 == (2 * pair + mxu) % 4) for mxu in range(2)]
            for k in range(groups):
                start(pair, k, same_rest)
                if not last and k == 1:
                    push(pair + 1)
                if k >= LAG:
                    finish(pair, k - LAG)
                elif not first:
                    finish(pair - 1, k - LAG + groups)

        push(0)
        work(0, True, False)
        pl.loop(1, NB // 2 - 1)(lambda pair: work(pair, False, False))
        work(NB // 2 - 1, False, True)
        for k in range(groups - LAG, groups):
            finish(NB // 2 - 1, k)

    def out_copy(k):
        at = pl.ds(pl.multiple_of(row_places[k] * OWN, OWN), OWN)
        return pltpu.make_async_copy(staged.at[k % 2], out_ref.at[:, at, :], sems.at[k % 2])

    def emit(g):
        if g >= 2:
            out_copy(g - 2).wait()
        for lag in range(HALF + 1):
            for h in range(2):
                e, o = (lagged[2 * (g % TOGETHER) + part][h, pl.ds(lag, OWN, stride=LAG_ROWS), :] for part in range(2))
                lanes = slice(h * 128, (h + 1) * 128)
                staged[g % 2, HALF + lag, :, lanes] = ((e + o) * (1.0 / math.sqrt(W * F))).astype(jnp.bfloat16)
                if lag:
                    staged[g % 2, HALF - lag, :, lanes] = ((e - o) * (1.0 / math.sqrt(W * F))).astype(jnp.bfloat16)
        out_copy(g).start()

    def lags_of(*accs):
        def acc_of(part, g, u):
            return accs[(part * TOGETHER + g % TOGETHER) * 4 + u % 4]

        def finish(g, u):
            for part in range(2):
                z = pltpu.matmul_pop(acc_of(part, g, u))
                for h in range(2):
                    rows_of = slice(u * LAG_ROWS, (u + 1) * LAG_ROWS)
                    lagged[2 * (g % TOGETHER) + part][h, rows_of, :] = z[:LAG_ROWS, h * 128 : (h + 1) * 128]

        for first in range(0, n_rows, TOGETHER):
            done = -1
            for t in range(OWN * F // 256):
                channels = [(k, u) for k, (tile, u) in enumerate(segments()) if tile == t]
                tables = [[table_ref[part, k] for part in range(2)] for k, _ in channels]
                for g in range(first, first + TOGETHER):
                    at = g * OWN * F + t * 256
                    staged_in = (t * TOGETHER + g) % 2
                    for part in range(2):
                        pltpu.matmul_push_rhs(cross[part, at : at + 256, :], staged_in, part)
                    for n, (k, u) in enumerate(channels):
                        for part in range(2):
                            pltpu.matmul_acc_lhs(acc_of(part, g, u), tables[n][part], None if n else staged_in)
                while done < channels[-1][1] - 2:
                    done += 1
                    for g in range(first, first + TOGETHER):
                        finish(g, done)
            for u in range(done + 1, OWN):
                for g in range(first, first + TOGETHER):
                    finish(g, u)
            for g in range(first, first + TOGETHER):
                emit(g)

    pl.run_scoped(cross_of, *[pltpu.ACC(mxu)((SOME * 16, 256), jnp.float32) for mxu in [0] * DEPTH + [1] * DEPTH])
    loads[-1].wait()
    pl.run_scoped(lags_of, *[pltpu.ACC(mxu)((LAG_TILE, 256), jnp.float32) for mxu in [0] * (4 * TOGETHER) + [1] * (4 * TOGETHER)])
    for k in range(n_rows - 2, n_rows):
        out_copy(k).wait()


def correlate(rows, cols, swapped, shape, kept=()):
    row_blocks, col_blocks = list(rows.values()), list(cols.values()) + [swapped[key] for key in cols]
    n, m = OWN * len(row_blocks), OWN * len(col_blocks)
    vmem, anywhere = pl.BlockSpec(memory_space=pltpu.VMEM), pl.BlockSpec(memory_space=pl.ANY)
    inputs = (*row_blocks, *col_blocks, jnp.asarray(lag_tables(), jnp.bfloat16), *kept)
    return pl.pallas_call(
        functools.partial(correlate_kernel, tuple(rows), tuple(cols), len(kept)),
        in_specs=[vmem] * len(row_blocks) + [anywhere] * (len(col_blocks) + 1 + len(kept)),
        out_specs=anywhere,
        out_shape=jax.ShapeDtypeStruct(shape, jnp.bfloat16),
        input_output_aliases={len(inputs) - 1: 0} if kept else {},
        scratch_shapes=[
            pltpu.VMEM((m, LANES), jnp.bfloat16),
            pltpu.VMEM((2, len(segments()), LAG_TILE, 256), jnp.bfloat16),
            pltpu.VMEM((n, LANES), jnp.float32),
            pltpu.VMEM((n, LANES), jnp.float32),
            pltpu.VMEM((2, n * F, m), jnp.bfloat16),
            *[pltpu.VMEM((2, OWN * LAG_ROWS, 128), jnp.float32)] * (2 * TOGETHER),
            pltpu.VMEM((2, LAGS, OWN, m), jnp.bfloat16),
            pltpu.SemaphoreType.DMA((2,)),
            pltpu.SemaphoreType.DMA((len(col_blocks) + 1,)),
        ],
        compiler_params=pltpu.CompilerParams(vmem_limit_bytes=50 * 1024 * 1024),
        cost_estimate=pl.CostEstimate(flops=n * 2 * 10**8, bytes_accessed=10**7, transcendentals=0),
    )(*inputs)


def near(block, side, move):
    return {(0, 0): block, (0, 1): side, (-1, 0): move(block, 1, 0), (1, 0): move(block, -1, 0)}


def far(found, move):
    return {
        (-1, 1): move(found[0, 1], 1, 0),
        (1, 1): move(found[0, 1], -1, 0),
        (2, 0): move(found[-1, 0], 1, 0),
        (2, 1): move(found[1, 0], -1, 1),
    }


def body(spectra, offsets, channel_mask):
    white = whiten(spectra, offsets, channel_mask)

    def over_rcv(value, ring, side):
        return lax.ppermute(value, "rcv", [(i, step(i, ring, side)) for i in range(8)])

    def over_src(value, ring, side):
        return lax.ppermute(value, "src", [(i, 2 * step(i // 2, ring, side) + i % 2) for i in range(16)])

    def other_core(value):
        return lax.ppermute(value, "src", [(i, i ^ 1) for i in range(16)])

    flip = [
        ((i * 2 + k) * 8 + step(j, 2, 0), (j * 2 + k) * 8 + i) for i in range(8) for k in range(2) for j in range(8)
    ]
    turned = lax.ppermute(white, ("src", "rcv"), flip)
    white, side, turned = lax.optimization_barrier((white, over_rcv(white, 0, 1), turned))
    cols = near(turned, over_src(turned, 0, 1), over_src)
    rows, cols = lax.optimization_barrier((near(white, side, over_rcv), cols))
    cols |= far(cols, over_src)
    swapped = {key: other_core(value) for key, value in cols.items()}
    shape = (LAGS, 8 * OWN, 16 * OWN)
    first = correlate(rows, cols, swapped, shape)
    return correlate(far(rows, over_rcv), cols, swapped, shape, (first,))


def solution(mesh):
    in_specs = (P(("src", "rcv"), None, None, None), P(("src", "rcv"), None), P(("src", "rcv")))
    out_specs = P(None, "src", "rcv")
    return jax.shard_map(body, mesh=mesh, in_specs=in_specs, out_specs=out_specs, check_vma=False)
```
